128 devices in a mesh: ha: 8 (over y_hi, z), wa: 16 (over y_lo, x, core).
Axes of the slice: x: 4, y: 4 (y_hi: 2, y_lo: 2; y = y_hi * 2 + y_lo), z: 4, core: 2. Of those that a mesh axis runs over, the one named last changes fastest.
Arguments:
- clip: bfloat16 [3, 17, 256, 512], P(None, None, 'ha', 'wa'), may hold values from -6 to 6
- w_first: bfloat16 [3, 3, 3, 3, 64], replicated, may hold values from -0.625 to 0.625
- b_first: float32 [64], replicated, may hold values from -3 to 3
- w_second: bfloat16 [3, 3, 3, 64, 128], replicated, may hold values from -0.15625 to 0.15625
- b_second: float32 [128], replicated, may hold values from -3 to 3
- upstream: bfloat16 [9, 128, 256, 128], P(None, 'ha', 'wa'), may hold values from -6 to 6
Outputs:
- input_grad: float32 [3, 17, 256, 512], P(None, None, 'ha', 'wa')
- grad_first: float32 [3, 3, 3, 3, 64], replicated
- grad_second: float32 [3, 3, 3, 64, 128], P(None, None, None, 'ha', 'wa')
The draws below stay inside these ranges and needn't reach their ends.
All inputs are finite; a program needn't handle non-finite values.
Results may differ from the reference program's by a relative error of at most 0.015.
The reference program's roundings to bfloat16 on the way (of `hidden`, `score_delta`, `hidden_delta`, `tangent` and `tangent_hidden`) count: a program that leaves them out, or rounds other values in their place, can miss the bound.
Values may be sent and summed in bfloat16 or wider, within the bound.
No kernel may reach another device: no remote copies, remote signals or barrier semaphores. Data moves between devices by JAX's collectives and lax.ppermute only.
A program may use at most 192 MiB of HBM per device.

```python
import jax
import jax.numpy as jnp
from jax import lax

C1 = 64
C2 = 128
FRAMES = 17
HEIGHT = 256
WIDTH = 512
FRAMES_OUT = 9


def steps_of(stream_key, shape, shards, least, high):
    gain = 1.0
    for dim, shards_of in shards:
        heights = jax.random.uniform(jax.random.fold_in(jax.random.fold_in(stream_key, 6), dim), (shards_of,), jnp.float32, least / len(shards), high / len(shards))
        gain = gain * jnp.repeat(jnp.exp(heights), shape[dim] // shards_of).reshape((-1,) + (1,) * (len(shape) - 1 - dim))
    return gain


def scatter_about(key, extent, scale, bound, split=(), kind=jnp.bfloat16):
    drawn = scale * jax.random.normal(key, extent, jnp.float32)
    if split:
        drawn = drawn * steps_of(key, extent, split, -0.22, 0.18)
    return jnp.clip(drawn, -bound, bound).astype(kind)


def setup_inputs(seed: int = 0) -> dict:
    seeds = jax.random.split(jax.random.key(seed), 7)
    return {
        "clip": scatter_about(seeds[0], (3, FRAMES, HEIGHT, WIDTH), 1.0, 6.0, ((2, 8), (3, 16))),
        "w_first": scatter_about(seeds[1], (3, 3, 3, 3, C1), 81 ** -0.5, 0.625),
        "b_first": scatter_about(seeds[2], (C1,), 0.5, 3.0, (), jnp.float32),
        "w_second": scatter_about(seeds[3], (3, 3, 3, C1, C2), (27 * C1) ** -0.5, 0.15625),
        "b_second": scatter_about(seeds[4], (C2,), 0.5, 3.0, (), jnp.float32),
        "upstream": scatter_about(seeds[5], (FRAMES_OUT, HEIGHT // 2, WIDTH // 2, C2), 1.0, 6.0, ((1, 8), (2, 16))),
    }


LEAK = 0.2


def convolve(source, kernel, specs, strides, padding, dilation):
    return lax.conv_general_dilated(source, kernel, strides, padding, lhs_dilation=dilation, dimension_numbers=specs, preferred_element_type=jnp.float32)


def tap_terms(source, cotangent, stride, channels_first):
    counts = cotangent.shape[:3]
    flat_cot = cotangent.reshape(-1, cotangent.shape[-1])
    pieces = []
    for depth_tap in range(3):
        for row_tap in range(3):
            for col_tap in range(3):
                offsets = (depth_tap, row_tap, col_tap)
                limits = tuple(offsets[k] + stride * (counts[k] - 1) + 1 for k in range(3))
                if channels_first:
                    piece = lax.slice(source, (0,) + offsets, (source.shape[0],) + limits, (1, stride, stride, stride))
                    pieces.append(jnp.dot(piece.reshape(source.shape[0], -1), flat_cot, preferred_element_type=jnp.float32))
                else:
                    piece = lax.slice(source, offsets + (0,), limits + (source.shape[3],), (stride, stride, stride, 1))
                    pieces.append(jnp.dot(piece.reshape(-1, source.shape[3]).T, flat_cot, preferred_element_type=jnp.float32))
    stacked = jnp.stack(pieces)
    return stacked.reshape(3, 3, 3, stacked.shape[1], stacked.shape[2])


def reference(clip, w_first, b_first, w_second, b_second, upstream):
    same = ((1, 1), (1, 1), (1, 1))
    unit = (1, 1, 1)
    pre_first = convolve(clip[None], w_first, ("NCDHW", "DHWIO", "NDHWC"), unit, same, unit)[0] + b_first
    slope_first = jnp.where(pre_first > 0, 1.0, LEAK)
    hidden = (pre_first * slope_first).astype(jnp.bfloat16)
    pre_second = convolve(hidden[None], w_second, ("NDHWC", "DHWIO", "NDHWC"), (2, 2, 2), same, unit)[0] + b_second
    slope_second = jnp.where(pre_second > 0, 1.0, LEAK)
    score_delta = (upstream.astype(jnp.float32) * slope_second).astype(jnp.bfloat16)
    back_hidden = convolve(score_delta[None], w_second[::-1, ::-1, ::-1], ("NDHWC", "DHWOI", "NDHWC"), unit, ((1, 1), (1, 2), (1, 2)), (2, 2, 2))[0]
    hidden_delta = (back_hidden * slope_first).astype(jnp.bfloat16)
    input_grad = convolve(hidden_delta[None], w_first[::-1, ::-1, ::-1], ("NDHWC", "DHWOI", "NCDHW"), unit, same, unit)[0]
    tangent = input_grad.astype(jnp.bfloat16)
    pre_tangent = convolve(tangent[None], w_first, ("NCDHW", "DHWIO", "NDHWC"), unit, same, unit)[0]
    tangent_hidden = (pre_tangent * slope_first).astype(jnp.bfloat16)
    scale = 1.0 / (FRAMES * HEIGHT * WIDTH)
    tangent_pad = jnp.pad(tangent, ((0, 0), (1, 1), (1, 1), (1, 1)))
    grad_first = tap_terms(tangent_pad, hidden_delta, 1, True) * scale
    hidden_pad = jnp.pad(tangent_hidden, ((1, 1), (1, 1), (1, 1), (0, 0)))
    grad_second = tap_terms(hidden_pad, score_delta, 2, False) * scale
    return input_grad, grad_first, grad_second
```

```python
import numpy as np
import jax
import jax.numpy as jnp
from jax import lax
from jax.experimental import pallas as pl
from jax.experimental.pallas import tpu as pltpu
from jax.sharding import PartitionSpec as P

LEAK = 0.2
T = 17
TO = 9
S = 24
F32 = jnp.float32
BF16 = jnp.bfloat16


def dot(a, b):
    return jnp.dot(a, b, preferred_element_type=F32)


def pick_columns():
    m = np.zeros((4, S, 48), np.float32)
    for d in range(4):
        for s in range(22):
            if 2 * s + d < 44:
                m[d, s, 2 * s + d] = 1
    return m.reshape(4 * S, 48)


def spread_rows():
    m = np.zeros((4, 144, 11, 2, 64), np.float32)
    for d in range(4):
        for q in range(22):
            for k in range(4):
                for ch in range(3):
                    if 2 * q + k < 44:
                        m[d, ch * 48 + 2 * q + k, q // 2, q % 2, k * 12 + d * 3 + ch] = 1
    return m.reshape(4, 144, 11 * 128)


def first_forward():
    m = np.zeros((3, 128, 2, 4, 81), np.float32)
    for a in range(3):
        for k in range(4):
            for d in range(4):
                for ch in range(3):
                    for rp in range(2):
                        for cp in range(2):
                            b, c = k - rp, d - cp
                            if 0 <= b < 3 and 0 <= c < 3:
                                tap = ((a * 3 + b) * 3 + c) * 3 + ch
                                lane = k * 12 + d * 3 + ch
                                m[a, lane, 0, rp * 2 + cp, tap] = 1
                                m[a, 64 + lane, 1, rp * 2 + cp, tap] = 1
    return m.reshape(384, 2, 4 * 81)


def first_backward():
    m = np.zeros((2, 2, 2, 2, 81, 128), np.float32)
    for di in range(2):
        for dj in range(2):
            for rp in range(2):
                for cp in range(2):
                    for ro in range(2):
                        for co in range(2):
                            b, c = ro + 2 - (2 * di + rp), co + 2 - (2 * dj + cp)
                            if 0 <= b < 3 and 0 <= c < 3:
                                for a in range(3):
                                    for ch in range(3):
                                        tap = ((a * 3 + b) * 3 + c) * 3 + ch
                                        m[di, dj, rp, cp, tap, a * 24 + ro * 12 + co * 3 + ch] = 1
    return m.reshape(16, 81, 128)


BLOCKS = ((1, 1), (1, 2), (2, 1), (2, 2), None, (1, 0), None, (2, 0), (0, 1), (0, 2), None, (0, 0))


def kernel(
    pos, clip, up, sel, spread, w1, b1, w2, b2, wb, wx,
    x_out, g_out,
    ct, p2, mk, sl, hf, h6, dacc, sdf, d4, dt, hdf, hd4, hds, ys, xf, tp, tpt, thf, th6, oacc, gacc, gf,
):
    r0, c0, rows, cols = pos[0], pos[1], pos[2], pos[3]

    def inside(r, c):
        return (r >= 0) & (r < rows) & (c >= 0) & (c < cols)

    sub = lax.broadcasted_iota(jnp.int32, (S, 256), 0)
    lane = lax.broadcasted_iota(jnp.int32, (S, 256), 1)
    for q in range(22):
        r = r0 + 2 * (q - 3) + (lane >> 7)
        c = c0 + 2 * (sub - 3) + ((lane >> 6) & 1)
        mk[q * S : (q + 1) * S, :] = jnp.where(inside(r, c), 1.0, 0.0)

    p2[0] = jnp.zeros(p2.shape[1:], F32)
    p2[T + 1] = jnp.zeros(p2.shape[1:], F32)
    ys[0] = jnp.zeros(ys.shape[1:], F32)
    ys[T + 1] = jnp.zeros(ys.shape[1:], F32)
    tp[0] = jnp.zeros(tp.shape[1:], BF16)
    tp[T + 1] = jnp.zeros(tp.shape[1:], BF16)
    tpt[0] = jnp.zeros(tpt.shape[1:], BF16)
    tpt[T + 1] = jnp.zeros(tpt.shape[1:], BF16)
    oacc[...] = jnp.zeros(oacc.shape, F32)
    gacc[...] = jnp.zeros(gacc.shape, F32)
    sdf[480:496, :] = jnp.zeros((16, 128), F32)
    xf[432:448, :] = jnp.zeros((16, 128), F32)
    gf[...] = jnp.zeros(gf.shape, F32)

    @pl.loop(0, T)
    def _(t):
        whole = jnp.concatenate([clip[0, t], clip[1, t], clip[2, t]], axis=0)
        turned = lax.dot_general(
            sel[...], whole, (((1,), (1,)), ((), ())), preferred_element_type=F32
        )
        at = pl.ds(pl.multiple_of(t * S, 8), S)
        for d in range(4):
            ct[d, at, :] = turned[d * S : (d + 1) * S]

    for n in range(0, 11, 2):
        width = min(2, 11 - n) * 128
        part = jnp.zeros((T * S, width), F32)
        for d in range(4):
            part += dot(ct[d].astype(BF16), spread[d, :, n * 128 : n * 128 + width])
        for k in range(width // 128):
            q = n + k
            p2[1 : T + 1, q * S : (q + 1) * S, :] = part[:, k * 128 : (k + 1) * 128].reshape(T, S, 128)

    for p in range(TO):
        dacc[p] = jnp.broadcast_to(b2[...], (480, 128))

    def forward(t):
        lhs = jnp.concatenate([p2[t], p2[t + 1], p2[t + 2]], axis=1).astype(BF16)
        pre = dot(lhs, w1[...]) + b1[...]
        slope = jnp.where(pre > 0, 1.0, LEAK)
        for q in range(11):
            for e in range(2):
                to = slice((2 * q + e) * S, (2 * q + e + 1) * S)
                of = (slice(q * S, (q + 1) * S), slice(e * 256, (e + 1) * 256))
                masked = slope[of] * mk[to, :]
                sl[t, to, :] = masked
                hf[to, :] = pre[of] * masked
        h6[:, 0:256] = hf[25:505, :].astype(BF16)
        h6[:, 256:512] = hf[24:504, :].astype(BF16)
        h6[:, 512:640] = hf[1:481, 128:256].astype(BF16)
        h6[:, 640:768] = hf[0:480, 128:256].astype(BF16)

    def even_forward(p):
        forward(2 * p)
        dacc[p] += dot(h6[...], w2[:, 256:384])

    @pl.loop(0, TO - 1)
    def _(p):
        even_forward(p)
        forward(2 * p + 1)
        both = dot(h6[...], w2[:, 0:256])
        dacc[p] += both[:, 0:128]
        dacc[p + 1] += both[:, 128:256]

    even_forward(TO - 1)

    at384 = lax.broadcasted_iota(jnp.int32, (384, 128), 0)
    core = jnp.where(at384 % S < 16, 1.0, 0.0)

    @pl.loop(0, TO)
    def _(p):
        slope = jnp.where(dacc[p] > 0, 1.0, LEAK)
        sdf[0:480, :] = up[p].astype(F32) * slope
        d4[p, :, 0:128] = sdf[0:464, :].astype(BF16)
        d4[p, :, 128:256] = sdf[1:465, :].astype(BF16)
        d4[p, :, 256:384] = sdf[24:488, :].astype(BF16)
        d4[p, :, 384:512] = sdf[25:489, :].astype(BF16)
        dt[p] = jnp.transpose(sdf[50:434, :] * core).astype(BF16)

    at416 = lax.broadcasted_iota(jnp.int32, (416, 256), 0)
    core_first = jnp.where(
        (at416 % S >= 1) & (at416 % S <= 16) & (at416 >= S) & (at416 < 17 * S), 1.0, 0.0
    )

    def backward(t, back):
        hdf[...] = back * sl[t, 25:489, :]
        hds[t] = (hdf[25:441, :] * core_first).astype(BF16)
        hd4[:, 0:256] = hdf[0:432, :].astype(BF16)
        hd4[:, 256:512] = hdf[1:433, :].astype(BF16)
        hd4[:, 512:768] = hdf[24:456, :].astype(BF16)
        hd4[:, 768:1024] = hdf[25:457, :].astype(BF16)
        ys[t + 1] = dot(hd4[...], wx[...])

    @pl.loop(0, TO - 1)
    def _(p):
        backward(2 * p, dot(d4[p], wb[0:512, :]))
        backward(2 * p + 1, dot(d4[p], wb[512:1024, :]) + dot(d4[p + 1], wb[1024:1536, :]))

    backward(2 * TO - 2, dot(d4[TO - 1], wb[0:512, :]))

    at432 = lax.broadcasted_iota(jnp.int32, (432, 128), 0)
    lane = lax.broadcasted_iota(jnp.int32, (432, 128), 1)
    second_row = lane >= 12
    in_row = jnp.where(second_row, lane - 12, lane)
    r = r0 + 2 * (at432 // S) - 3 + jnp.where(second_row, 1, 0)
    c = c0 + 2 * (at432 % S) - 3 + jnp.where(in_row >= 3, 1, 0)
    live = inside(r, c) & (in_row < 6)

    @pl.loop(0, T)
    def _(t):
        x = ys[t + 2] + pltpu.roll(ys[t + 1], 104, 1) + pltpu.roll(ys[t], 80, 1)
        x_out[t] = x[:, 0:S]
        xf[0:432, :] = jnp.where(live, x, 0.0)
        wide = (
            xf[0:416, :]
            + pltpu.roll(xf[1:417, :], 6, 1)
            + pltpu.roll(xf[24:440, :], 24, 1)
            + pltpu.roll(xf[25:441, :], 30, 1)
        )
        tp[t + 1] = wide.astype(BF16)
        tpt[t + 1] = jnp.transpose(wide)[0:48].astype(BF16)

    def tangents(t):
        lhs = jnp.concatenate([tp[t], tp[t + 1], tp[t + 2]], axis=1)
        thf[...] = dot(lhs, w1[:, 0:256]) * sl[t, 50:466, :]
        th6[:, 0:256] = thf[25:409, :].astype(BF16)
        th6[:, 256:512] = thf[24:408, :].astype(BF16)
        th6[:, 512:640] = thf[1:385, 128:256].astype(BF16)
        th6[:, 640:768] = thf[0:384, 128:256].astype(BF16)
        turned = jnp.concatenate([tpt[t], tpt[t + 1], tpt[t + 2]], axis=0)
        gacc[...] += dot(turned, hds[t])

    @pl.loop(0, TO - 1)
    def _(p):
        tangents(2 * p)
        oacc[128:256, :] += dot(dt[p], th6[...])
        tangents(2 * p + 1)
        oacc[256:384, :] += dot(dt[p], th6[...])
        oacc[0:128, :] += dot(dt[p + 1], th6[...])

    tangents(2 * TO - 2)
    oacc[128:256, :] += dot(dt[TO - 1], th6[...])

    for a in range(3):
        for b in range(3):
            total = jnp.zeros((9, 64), F32)
            for rp in range(2):
                for cp in range(2):
                    start = a * 48 + (b + rp) * 12 + cp * 3
                    part = (rp * 2 + cp) * 64
                    total += gacc[start : start + 9, part : part + 64]
            gf[a * 27 + b * 9 : a * 27 + b * 9 + 9, :] = total
    flat = jnp.concatenate([gf[k * 8 : (k + 1) * 8, :] for k in range(12)], axis=1)
    for w in range(16):
        for a in range(3):
            g_out[w, a * 8 : (a + 1) * 8, :] = oacc[a * 128 + w * 8 : a * 128 + w * 8 + 8, :]
        g_out[w, 24:32, :] = flat


def run_kernel(*args):
    vm = lambda shape, kind=F32: pltpu.VMEM(shape, kind)
    vmem = pl.BlockSpec(memory_space=pltpu.VMEM)
    return pl.pallas_call(
        kernel,
        out_shape=(
            jax.ShapeDtypeStruct((T, 432, S), F32),
            jax.ShapeDtypeStruct((16, 32, 768), F32),
        ),
        in_specs=[pl.BlockSpec(memory_space=pltpu.SMEM)] + [vmem] * 10,
        out_specs=(vmem, vmem),
        scratch_shapes=[
            vm((4, T * S, 144)),
            vm((T + 2, 264, 128)),
            vm((528, 256)),
            vm((T, 528, 256)),
            vm((528, 256)),
            vm((480, 768), BF16),
            vm((TO, 480, 128)),
            vm((496, 128)),
            vm((TO, 464, 512), BF16),
            vm((TO, 128, 384), BF16),
            vm((464, 256)),
            vm((432, 1024), BF16),
            vm((T, 416, 256), BF16),
            vm((T + 2, 432, 128)),
            vm((448, 128)),
            vm((T + 2, 416, 128), BF16),
            vm((T + 2, 48, 416), BF16),
            vm((416, 256)),
            vm((384, 768), BF16),
            vm((384, 768)),
            vm((144, 256)),
            vm((96, 64)),
        ],
        compiler_params=pltpu.CompilerParams(vmem_limit_bytes=60 * 1024 * 1024),
        cost_estimate=pl.CostEstimate(flops=10**10, bytes_accessed=2 * 10**7, transcendentals=0),
    )(*args)


def shifted(value, axis, by):
    size = lax.axis_size(axis)
    pairs = [(i, i + by) for i in range(size) if 0 <= i + by < size]
    return lax.ppermute(value, axis, pairs)


def around(value, axis, dim, before, after):
    length = value.shape[dim]
    low = shifted(lax.slice_in_dim(value, length - before, length, axis=dim), axis, 1)
    high = shifted(lax.slice_in_dim(value, 0, after, axis=dim), axis, -1)
    return jnp.concatenate([low, value, high], axis=dim)


def body(clip, w_first, b_first, w_second, b_second, upstream):
    rows = clip.shape[2] * lax.axis_size("ha")
    cols = clip.shape[3] * lax.axis_size("wa")
    ha, wa = lax.axis_index("ha"), lax.axis_index("wa")
    pos = jnp.stack([ha * 32, wa * 32, jnp.int32(rows), jnp.int32(cols)]).astype(jnp.int32)

    clip_ext = around(around(clip, "ha", 2, 7, 5), "wa", 3, 7, 5)
    clip_ext = jnp.pad(clip_ext, ((0, 0), (0, 0), (0, 4), (0, 4)))
    up = around(around(upstream, "ha", 1, 2, 2), "wa", 2, 2, 2)
    up = jnp.pad(up, ((0, 0), (0, 0), (0, 4), (0, 0))).reshape(TO, 480, 128)

    w_flat = w_first.reshape(81, 64)
    diagonal = jnp.concatenate(
        [jnp.pad(w_flat, ((0, 0), (64 * k, 192 - 64 * k))) for k in range(4)], axis=0
    )
    forward_pick = jnp.asarray(first_forward(), BF16)
    w1 = jnp.concatenate(
        [dot(forward_pick[:, e], diagonal).astype(BF16) for e in range(2)], axis=1
    )
    b1 = jnp.tile(b_first, 8)[None]
    wx = jnp.einsum(
        "ko,bkl->bol", w_flat, jnp.asarray(first_backward(), BF16), preferred_element_type=F32
    )
    wx = wx.astype(BF16).reshape(1024, 128)
    nothing = jnp.zeros((64, 128), BF16)
    w2 = jnp.concatenate(
        [
            jnp.concatenate(
                [nothing if k is None else w_second[a, k[0], k[1]] for k in BLOCKS], axis=0
            )
            for a in (2, 0, 1)
        ],
        axis=1,
    )
    turned = jnp.swapaxes(w_second, 3, 4)
    blank = jnp.zeros((128, 64), BF16)
    pieces = []
    for a in (1, 2, 0):
        for dq in range(2):
            for ds in range(2):
                line = []
                for rp in range(2):
                    for cp in range(2):
                        b, c = rp + 1 - 2 * dq, cp + 1 - 2 * ds
                        line.append(turned[a, b, c] if b >= 0 and c >= 0 else blank)
                pieces.append(jnp.concatenate(line, axis=1))
    wb = jnp.concatenate(pieces, axis=0)

    x_out, g_out = run_kernel(
        pos,
        clip_ext,
        up,
        jnp.asarray(pick_columns(), BF16),
        jnp.asarray(spread_rows(), BF16),
        w1,
        b1,
        w2,
        b_second[None],
        wb,
        wx,
    )

    scale = 1.0 / (T * rows * cols)
    size_w, size_h = lax.axis_size("wa"), lax.axis_size("ha")
    part = lax.all_to_all(g_out.astype(BF16), "wa", 0, 0, tiled=True)
    part = part.astype(F32).sum(0) * scale
    second = part[0:24].reshape(3, 8, 12, 8, 8)
    keep = [BLOCKS.index((b, c)) for b in range(3) for c in range(3)]
    second = jnp.stack([second[:, :, k] for k in keep], axis=0)
    second = second.transpose(3, 0, 1, 2, 4).reshape(8, 9 * 3 * 8 * 8)
    first = jnp.broadcast_to(part[24:32].reshape(1, 6144), (8, 6144))
    both = lax.all_to_all(jnp.concatenate([second, first], axis=1), "ha", 0, 0, tiled=True).sum(0)
    grad_second = both[:1728].reshape(3, 3, 3, 8, 8).transpose(2, 0, 1, 4, 3)
    grad_first = both[1728:].reshape(8, 12, 64).transpose(1, 0, 2).reshape(96, 64)[:81]
    grad_first = grad_first.reshape(3, 3, 3, 3, 64)

    x = x_out.reshape(T, 18, S, 2, 12)[:, :, :, :, :6].reshape(T, 18, S, 2, 2, 3)
    x = x.transpose(5, 0, 1, 3, 2, 4).reshape(3, T, 36, 48)
    input_grad = x[:, :, 3:35, 3:35]
    return (input_grad, grad_first, grad_second)


def solution(mesh):
    placed = (P(None, None, "ha", "wa"), P(), P(), P(), P(), P(None, "ha", "wa", None))
    return jax.shard_map(
        body,
        mesh=mesh,
        in_specs=placed,
        out_specs=(P(None, None, "ha", "wa"), P(), P(None, None, None, "ha", "wa")),
        check_vma=False,
    )
```

```python
import numpy as np
import jax
import jax.numpy as jnp
from jax import lax
from jax.experimental import pallas as pl
from jax.experimental.pallas import tpu as pltpu
from jax.sharding import PartitionSpec as P

LEAK = 0.2
T = 17
TO = 9
S = 24
F32 = jnp.float32
BF16 = jnp.bfloat16


def dot(a, b):
    return jnp.dot(a, b, preferred_element_type=F32)


def dot_nt(a, b):
    return lax.dot_general(a, b, (((1,), (1,)), ((), ())), preferred_element_type=F32)


def pick_columns():
    m = np.zeros((4, S, 48), np.float32)
    for d in range(4):
        for s in range(22):
            m[d, s, 2 * s + d + 1] = 1
    m = m.reshape(4 * S, 48)
    return m[:, 8:40], m[:, :8], m[:, 40:]


def place_columns():
    m = np.zeros((2, 512, 18, 32), np.float32)
    for p in range(18):
        for s in range(18):
            for co in range(2):
                if 0 <= 2 * s - 3 + co < 32:
                    m[co, p * S + s, p, 2 * s - 3 + co] = 1
    return m.reshape(1024, 576)


def spread_rows():
    m = np.zeros((4, 144, 11, 2, 64), np.float32)
    for d in range(4):
        for q in range(22):
            for k in range(4):
                for ch in range(3):
                    if 2 * q + k + 1 < 48:
                        m[d, ch * 48 + 2 * q + k + 1, q // 2, q % 2, k * 12 + d * 3 + ch] = 1
    return m.reshape(4, 144, 11 * 128)


def first_forward():
    m = np.zeros((3, 128, 2, 4, 81), np.float32)
    for a in range(3):
        for k in range(4):
            for d in range(4):
                for ch in range(3):
                    for rp in range(2):
                        for cp in range(2):
                            b, c = k - rp, d - cp
                            if 0 <= b < 3 and 0 <= c < 3:
                                tap = ((a * 3 + b) * 3 + c) * 3 + ch
                                lane = k * 12 + d * 3 + ch
                                m[a, lane, 0, rp * 2 + cp, tap] = 1
                                m[a, 64 + lane, 1, rp * 2 + cp, tap] = 1
    return m.reshape(384, 2, 4 * 81)


def first_backward():
    m = np.zeros((2, 2, 2, 2, 81, 80), np.float32)
    for di in range(2):
        for dj in range(2):
            for rp in range(2):
                for cp in range(2):
                    for ro in range(2):
                        for co in range(2):
                            b, c = ro + 2 - (2 * di + rp), co + 2 - (2 * dj + cp)
                            if 0 <= b < 3 and 0 <= c < 3:
                                for a in range(3):
                                    for ch in range(3):
                                        tap = ((a * 3 + b) * 3 + c) * 3 + ch
                                        m[di, dj, rp, cp, tap, a * 24 + ro * 12 + co * 3 + ch] = 1
    return m.reshape(16, 81, 80)


BLOCKS = ((1, 1), (1, 2), (2, 1), (2, 2), None, (1, 0), None, (2, 0), (0, 1), (0, 2), None, (0, 0))


def kernel(
    pos, clip, side, up, sel_mid, sel_side, spread, w1, b1, w2, b2, wb, wx, place,
    x_out, g_out,
    ct, p2, mk, sl, hf_a, hf_b, h6_a, h6_b, dacc, sdf, d4, dt, hdf_a, hdf_b, hd4_a, hd4_b, hds, yt, xs, tp, tpt,
    thf_a, thf_b, th6_a, th6_b, oacc, gacc, gf,
):
    r0, c0, rows, cols = pos[0], pos[1], pos[2], pos[3]

    def inside(r, c):
        return (r >= 0) & (r < rows) & (c >= 0) & (c < cols)

    sub = lax.broadcasted_iota(jnp.int32, (S, 256), 0)
    lane = lax.broadcasted_iota(jnp.int32, (S, 256), 1)
    for q in range(22):
        r = r0 + 2 * (q - 3) + (lane >> 7)
        c = c0 + 2 * (sub - 3) + ((lane >> 6) & 1)
        mk[q * S : (q + 1) * S, :] = jnp.where(inside(r, c), 1.0, 0.0)

    p2[0] = jnp.zeros(p2.shape[1:], F32)
    p2[T + 1] = jnp.zeros(p2.shape[1:], F32)
    yt[...] = jnp.zeros(yt.shape, F32)
    tp[...] = jnp.zeros(tp.shape, BF16)
    tpt[0] = jnp.zeros(tpt.shape[1:], BF16)
    tpt[T + 1] = jnp.zeros(tpt.shape[1:], BF16)
    oacc[...] = jnp.zeros(oacc.shape, F32)
    gacc[...] = jnp.zeros(gacc.shape, F32)
    sdf[480:496, :] = jnp.zeros((16, 128), F32)
    gf[...] = jnp.zeros(gf.shape, F32)
    h6_b[...] = jnp.zeros(h6_b.shape, BF16)
    hd4_b[...] = jnp.zeros(hd4_b.shape, BF16)
    th6_b[...] = jnp.zeros(th6_b.shape, BF16)

    @pl.loop(0, T)
    def _(t):
        middle = jnp.concatenate([clip[0, t], clip[1, t], clip[2, t]], axis=0)
        edges = jnp.concatenate([side[0, t], side[1, t], side[2, t]], axis=1)
        turned = dot_nt(sel_mid[...], middle) + dot(sel_side[...], edges)
        at = pl.ds(pl.multiple_of(t * S, 8), S)
        for d in range(4):
            ct[d, at, :] = turned[d * S : (d + 1) * S]

    for n in range(0, 11, 2):
        width = min(2, 11 - n) * 128
        part = jnp.zeros((T * S, width), F32)
        for d in range(4):
            part += dot(ct[d].astype(BF16), spread[d, :, n * 128 : n * 128 + width])
        for k in range(width // 128):
            q = n + k
            p2[1 : T + 1, q * S : (q + 1) * S, :] = part[:, k * 128 : (k + 1) * 128].reshape(T, S, 128)

    for p in range(TO + 1):
        dacc[p] = jnp.broadcast_to(b2[...], (480, 128))

    def hidden(t, hf, h6):
        lhs = jnp.concatenate([p2[t], p2[t + 1], p2[t + 2]], axis=1).astype(BF16)
        pre = dot(lhs, w1[...]) + b1[...]
        slope = jnp.where(pre > 0, 1.0, LEAK)
        for q in range(11):
            for e in range(2):
                to = slice((2 * q + e) * S, (2 * q + e + 1) * S)
                of = (slice(q * S, (q + 1) * S), slice(e * 256, (e + 1) * 256))
                masked = slope[of] * mk[to, :]
                sl[t, to, :] = masked
                hf[to, :] = pre[of] * masked
        h6[:, 0:256] = hf[25:505, :].astype(BF16)
        h6[:, 256:512] = hf[24:504, :].astype(BF16)
        h6[:, 512:640] = hf[1:481, 128:256].astype(BF16)
        h6[:, 640:768] = hf[0:480, 128:256].astype(BF16)

    def odd_second(p):
        both = dot(h6_b[...], w2[:, 0:256])
        dacc[p + 1] += both[:, 0:128]
        dacc[p + 2] += both[:, 128:256]

    def even_second(p):
        dacc[p + 1] += dot(h6_a[...], w2[:, 256:384])

    @pl.loop(0, TO - 1)
    def _(p):
        hidden(2 * p, hf_a, h6_a)
        odd_second(p - 1)
        hidden(2 * p + 1, hf_b, h6_b)
        even_second(p)

    hidden(2 * TO - 2, hf_a, h6_a)
    odd_second(TO - 2)
    even_second(TO - 1)

    at384 = lax.broadcasted_iota(jnp.int32, (384, 128), 0)
    core = jnp.where(at384 % S < 16, 1.0, 0.0)

    @pl.loop(0, TO)
    def _(p):
        slope = jnp.where(dacc[p + 1] > 0, 1.0, LEAK)
        sdf[0:480, :] = up[p].astype(F32) * slope
        d4[p, :, 0:128] = sdf[0:464, :].astype(BF16)
        d4[p, :, 128:256] = sdf[1:465, :].astype(BF16)
        d4[p, :, 256:384] = sdf[24:488, :].astype(BF16)
        d4[p, :, 384:512] = sdf[25:489, :].astype(BF16)
        dt[p] = jnp.transpose(sdf[50:434, :] * core).astype(BF16)

    at416 = lax.broadcasted_iota(jnp.int32, (416, 256), 0)
    core_first = jnp.where(
        (at416 % S >= 1) & (at416 % S <= 16) & (at416 >= S) & (at416 < 17 * S), 1.0, 0.0
    )

    def delta(t, back, hdf, hd4):
        hdf[...] = back * sl[t, 25:489, :]
        hds[t] = (hdf[25:441, :] * core_first).astype(BF16)
        hd4[:, 0:256] = hdf[0:432, :].astype(BF16)
        hd4[:, 256:512] = hdf[1:433, :].astype(BF16)
        hd4[:, 512:768] = hdf[24:456, :].astype(BF16)
        hd4[:, 768:1024] = hdf[25:457, :].astype(BF16)

    def products(t, hd4):
        yt[t + 2, :, 0:432] = dot_nt(wx[...], hd4[...])

    @pl.loop(0, TO - 1)
    def _(p):
        delta(2 * p, dot(d4[p], wb[0:512, :]), hdf_a, hd4_a)
        products(2 * p - 1, hd4_b)
        back = dot(d4[p], wb[512:1024, :]) + dot(d4[p + 1], wb[1024:1536, :])
        delta(2 * p + 1, back, hdf_b, hd4_b)
        products(2 * p, hd4_a)

    delta(2 * TO - 2, dot(d4[TO - 1], wb[0:512, :]), hdf_a, hd4_a)
    products(2 * TO - 3, hd4_b)
    products(2 * TO - 2, hd4_a)

    index = lax.broadcasted_iota(jnp.int32, (S, 512), 0)
    cell = lax.broadcasted_iota(jnp.int32, (S, 512), 1)
    second_row = index >= 12
    in_row = jnp.where(second_row, index - 12, index)
    r = r0 + 2 * (cell // S) - 3 + jnp.where(second_row, 1, 0)
    c = c0 + 2 * (cell % S) - 3 + jnp.where(in_row >= 3, 1, 0)
    live = inside(r, c) & (in_row < 6) & (cell < 432)

    @pl.loop(0, T)
    def _(t):
        x = yt[t + 3, 0:24, :] + yt[t + 2, 24:48, :] + yt[t + 1, 48:72, :]
        at = pl.ds(pl.multiple_of(t * 48, 16), 48)
        for co in range(2):
            here = x if co == 0 else pltpu.roll(x, 21, 0)
            high = here.astype(BF16).astype(F32)
            xs[at, co * 512 : (co + 1) * 512] = jnp.concatenate([high, here - high], axis=0).astype(BF16)
        m = jnp.where(live, x, 0.0)
        upper = m + pltpu.roll(pltpu.roll(m, 511, 1), 6, 0)
        lower = pltpu.roll(m, 488, 1) + pltpu.roll(pltpu.roll(m, 487, 1), 6, 0)
        wide = jnp.concatenate([upper, lower], axis=0)
        tpt[t + 1] = wide[:, 0:416].astype(BF16)
        tp[t + 1, :, 0:48] = jnp.transpose(wide)[0:416].astype(BF16)

    for n in range(T):
        placed = dot(xs[n * 48 : (n + 1) * 48, :], place[...])
        placed = placed[0:24] + placed[24:48]
        for p in range(18):
            for ro in range(2):
                row = 2 * p - 3 + ro
                if 0 <= row < 32:
                    for ch in range(3):
                        k = ro * 12 + ch
                        x_out[ch, n, row : row + 1, :] = placed[k : k + 1, p * 32 : p * 32 + 32]

    def tangents(t, thf, th6):
        lhs = jnp.concatenate([tp[t], tp[t + 1], tp[t + 2]], axis=1)
        thf[...] = dot(lhs, w1[:, 0:256]) * sl[t, 50:466, :]
        th6[:, 0:256] = thf[25:409, :].astype(BF16)
        th6[:, 256:512] = thf[24:408, :].astype(BF16)
        th6[:, 512:640] = thf[1:385, 128:256].astype(BF16)
        th6[:, 640:768] = thf[0:384, 128:256].astype(BF16)
        turned = jnp.concatenate([tpt[t], tpt[t + 1], tpt[t + 2]], axis=0)
        gacc[...] += dot(turned, hds[t])

    def odd_terms(p):
        oacc[256:384, :] += dot(dt[jnp.maximum(p, 0)], th6_b[...])
        oacc[0:128, :] += dot(dt[p + 1], th6_b[...])

    def even_terms(p):
        oacc[128:256, :] += dot(dt[p], th6_a[...])

    @pl.loop(0, TO - 1)
    def _(p):
        tangents(2 * p, thf_a, th6_a)
        odd_terms(p - 1)
        tangents(2 * p + 1, thf_b, th6_b)
        even_terms(p)

    tangents(2 * TO - 2, thf_a, th6_a)
    odd_terms(TO - 2)
    even_terms(TO - 1)

    for a in range(3):
        for b in range(3):
            total = jnp.zeros((9, 64), F32)
            for rp in range(2):
                for cp in range(2):
                    start = a * 48 + (b + rp) * 12 + cp * 3
                    part = (rp * 2 + cp) * 64
                    total += gacc[start : start + 9, part : part + 64]
            gf[a * 27 + b * 9 : a * 27 + b * 9 + 9, :] = total

    left_half = lax.broadcasted_iota(jnp.int32, (8, 128), 1) < 64
    ends = jnp.concatenate([gf[24:56, :], gf[53:85, :]], axis=1)
    ends = jnp.concatenate([ends, jnp.zeros((8, 128), F32)], axis=0)
    start = jnp.concatenate([gf[0:24, :], jnp.zeros((24, 64), F32)], axis=1)
    for w in range(16):
        tiles = [[oacc[a * 128 + w * 8 : a * 128 + w * 8 + 8, k * 128 : k * 128 + 128] for a in range(3)] for k in range(6)]
        mixed = [jnp.where(left_half, pltpu.roll(tiles[2][a], 64, 1), tiles[3][a]) for a in range(3)]
        last = [jnp.where(left_half, start[a * 8 : a * 8 + 8], tiles[5][a]) for a in range(3)]
        g_out[w] = jnp.concatenate(tiles[0] + tiles[1] + mixed + tiles[4] + last + [ends], axis=0).astype(BF16)


TAPS = ((1, 1), (1, 2), (2, 1), (2, 2), (1, 0), (2, 0), (0, 1), (0, 2), None, (0, 0))


def run_kernel(*args):
    vm = lambda shape, kind=F32: pltpu.VMEM(shape, kind)
    vmem = pl.BlockSpec(memory_space=pltpu.VMEM)
    return pl.pallas_call(
        kernel,
        out_shape=(
            jax.ShapeDtypeStruct((3, T, 32, 32), F32),
            jax.ShapeDtypeStruct((16, 160, 128), BF16),
        ),
        in_specs=[pl.BlockSpec(memory_space=pltpu.SMEM)] + [vmem] * 13,
        out_specs=(vmem, vmem),
        scratch_shapes=[
            vm((4, T * S, 144)),
            vm((T + 2, 264, 128)),
            vm((528, 256)),
            vm((T, 528, 256)),
            vm((528, 256)),
            vm((528, 256)),
            vm((480, 768), BF16),
            vm((480, 768), BF16),
            vm((TO + 1, 480, 128)),
            vm((496, 128)),
            vm((TO, 464, 512), BF16),
            vm((TO, 128, 384), BF16),
            vm((464, 256)),
            vm((464, 256)),
            vm((432, 1024), BF16),
            vm((432, 1024), BF16),
            vm((T, 416, 256), BF16),
            vm((T + 3, 80, 512)),
            vm((T * 48, 1024), BF16),
            vm((T + 2, 416, 128), BF16),
            vm((T + 2, 48, 416), BF16),
            vm((416, 256)),
            vm((416, 256)),
            vm((384, 768), BF16),
            vm((384, 768), BF16),
            vm((384, 768)),
            vm((144, 256)),
            vm((96, 64)),
        ],
        compiler_params=pltpu.CompilerParams(vmem_limit_bytes=60 * 1024 * 1024),
        cost_estimate=pl.CostEstimate(flops=10**10, bytes_accessed=2 * 10**7, transcendentals=0),
    )(*args)


def swapped(to_next, to_prev, axis):
    size, at = lax.axis_size(axis), lax.axis_index(axis)
    ring = [(i, (i + 1) % size) for i in range(size)]
    before = lax.ppermute(to_next, axis, ring)
    after = lax.ppermute(to_prev, axis, [(j, i) for i, j in ring])
    nothing = jnp.zeros_like(before)
    return jnp.where(at > 0, before, nothing), jnp.where(at < size - 1, after, nothing)


def packed(clip_part, up_part):
    flat = clip_part.reshape(408, clip_part.shape[3])
    flat = jnp.pad(flat, ((0, 0), (0, 128 - flat.shape[1])))
    return jnp.concatenate([flat, up_part.reshape(-1, 128)], axis=0)


def body(clip, w_first, b_first, w_second, b_second, upstream):
    rows = clip.shape[2] * lax.axis_size("ha")
    cols = clip.shape[3] * lax.axis_size("wa")
    ha, wa = lax.axis_index("ha"), lax.axis_index("wa")
    pos = jnp.stack([ha * 32, wa * 32, jnp.int32(rows), jnp.int32(cols)]).astype(jnp.int32)

    above, below = swapped(
        packed(clip[:, :, 24:32], upstream[:, 14:16]), packed(clip[:, :, 0:8], upstream[:, 0:2]), "ha"
    )
    clip_part = lambda v, width: v[:408, :width].reshape(3, T, 8, width)
    clip_rows = jnp.concatenate([clip_part(above, 32), clip, clip_part(below, 32)], axis=2)
    up_part = lambda v: v[408:].reshape(TO, 2, 16, 128)
    up_rows = jnp.concatenate([up_part(above), upstream, up_part(below)], axis=1)
    left, right = swapped(
        packed(jnp.swapaxes(clip_rows[:, :, :, 24:32], 2, 3), up_rows[:, :, 14:16]),
        packed(jnp.swapaxes(clip_rows[:, :, :, 0:8], 2, 3), up_rows[:, :, 0:2]),
        "wa",
    )
    side = jnp.concatenate([clip_part(left, 48), clip_part(right, 48)], axis=2)
    up_part = lambda v: v[408:].reshape(TO, 20, 2, 128)
    spare = jnp.zeros((TO, 20, 4, 128), BF16)
    up = jnp.concatenate([up_part(left), up_rows, up_part(right), spare], axis=2).reshape(TO, 480, 128)

    w_flat = w_first.reshape(81, 64)
    diagonal = jnp.concatenate(
        [jnp.pad(w_flat, ((0, 0), (64 * k, 192 - 64 * k))) for k in range(4)], axis=0
    )
    forward_pick = jnp.asarray(first_forward(), BF16)
    w1 = jnp.concatenate(
        [dot(forward_pick[:, e], diagonal).astype(BF16) for e in range(2)], axis=1
    )
    b1 = jnp.tile(b_first, 8)[None]
    wx = jnp.einsum(
        "ko,bkl->lbo", w_flat, jnp.asarray(first_backward(), BF16), preferred_element_type=F32
    )
    wx = wx.astype(BF16).reshape(80, 1024)
    nothing = jnp.zeros((64, 128), BF16)
    w2 = jnp.concatenate(
        [
            jnp.concatenate(
                [nothing if k is None else w_second[a, k[0], k[1]] for k in BLOCKS], axis=0
            )
            for a in (2, 0, 1)
        ],
        axis=1,
    )
    turned = jnp.swapaxes(w_second, 3, 4)
    blank = jnp.zeros((128, 64), BF16)
    pieces = []
    for a in (1, 2, 0):
        for dq in range(2):
            for ds in range(2):
                line = []
                for rp in range(2):
                    for cp in range(2):
                        b, c = rp + 1 - 2 * dq, cp + 1 - 2 * ds
                        line.append(turned[a, b, c] if b >= 0 and c >= 0 else blank)
                pieces.append(jnp.concatenate(line, axis=1))
    wb = jnp.concatenate(pieces, axis=0)

    middle, first8, last8 = pick_columns()
    input_grad, terms = run_kernel(
        pos,
        clip_rows,
        side,
        up,
        jnp.asarray(middle, BF16),
        jnp.asarray(np.concatenate([first8, last8], axis=1), BF16),
        jnp.asarray(spread_rows(), BF16),
        w1,
        b1,
        w2,
        b_second[None],
        wb,
        wx,
        jnp.asarray(place_columns(), BF16),
    )

    scale = 1.0 / (T * rows * cols)
    part = lax.all_to_all(terms, "wa", 0, 0, tiled=True)
    part = part.astype(F32).sum(0) * scale
    second = part[0:120].reshape(120, 2, 8, 8).transpose(2, 0, 1, 3).reshape(8, 15, 128)
    first = jnp.broadcast_to(part[96:160], (8, 64, 128))
    both = lax.all_to_all(jnp.concatenate([second, first], axis=1), "ha", 0, 0, tiled=True).sum(0)
    second = both[:15].reshape(5, 3, 8, 2, 8)
    keep = [TAPS.index((b, c)) for b in range(3) for c in range(3)]
    second = second.transpose(0, 3, 1, 4, 2).reshape(10, 3, 8, 8)
    grad_second = jnp.stack([second[k] for k in keep], axis=1).reshape(3, 3, 3, 8, 8)
    first = both[15:]
    grad_first = jnp.concatenate([first[0:24, 0:64], first[24:53, 0:64], first[24:53, 64:128]], axis=0)
    grad_first = grad_first[:81].reshape(3, 3, 3, 3, 64)
    return (input_grad, grad_first, grad_second)


def solution(mesh):
    placed = (P(None, None, "ha", "wa"), P(), P(), P(), P(), P(None, "ha", "wa", None))
    return jax.shard_map(
        body,
        mesh=mesh,
        in_specs=placed,
        out_specs=(P(None, None, "ha", "wa"), P(), P(None, None, None, "ha", "wa")),
        check_vma=False,
    )
```

```python
import numpy as np
import jax
import jax.numpy as jnp
from jax import lax
from jax.experimental import pallas as pl
from jax.experimental.pallas import tpu as pltpu
from jax.sharding import PartitionSpec as P

LEAK = 0.2
T = 17
TO = 9
S = 24
F32 = jnp.float32
BF16 = jnp.bfloat16


def dot(a, b):
    return jnp.dot(a, b, preferred_element_type=F32)


def dot_nt(a, b):
    return lax.dot_general(a, b, (((1,), (1,)), ((), ())), preferred_element_type=F32)


def pick_columns():
    m = np.zeros((4, S, 48), np.float32)
    for d in range(4):
        for s in range(22):
            m[d, s, 2 * s + d + 1] = 1
    m = m.reshape(4 * S, 48)
    return m[:, 8:40], m[:, :8], m[:, 40:]


def place_columns():
    m = np.zeros((2, 512, 18, 32), np.float32)
    for p in range(18):
        for s in range(18):
            for co in range(2):
                if 0 <= 2 * s - 3 + co < 32:
                    m[co, p * S + s, p, 2 * s - 3 + co] = 1
    return m.reshape(1024, 576)


def spread_rows():
    m = np.zeros((4, 144, 11, 2, 64), np.float32)
    for d in range(4):
        for q in range(22):
            for k in range(4):
                for ch in range(3):
                    if 2 * q + k + 1 < 48:
                        m[d, ch * 48 + 2 * q + k + 1, q // 2, q % 2, k * 12 + d * 3 + ch] = 1
    return m.reshape(4, 144, 11 * 128)


def first_forward():
    m = np.zeros((3, 128, 2, 4, 81), np.float32)
    for a in range(3):
        for k in range(4):
            for d in range(4):
                for ch in range(3):
                    for rp in range(2):
                        for cp in range(2):
                            b, c = k - rp, d - cp
                            if 0 <= b < 3 and 0 <= c < 3:
                                tap = ((a * 3 + b) * 3 + c) * 3 + ch
                                lane = k * 12 + d * 3 + ch
                                m[a, lane, 0, rp * 2 + cp, tap] = 1
                                m[a, 64 + lane, 1, rp * 2 + cp, tap] = 1
    return m.reshape(384, 2, 4 * 81)


def first_backward():
    m = np.zeros((2, 2, 2, 2, 81, 80), np.float32)
    for di in range(2):
        for dj in range(2):
            for rp in range(2):
                for cp in range(2):
                    for ro in range(2):
                        for co in range(2):
                            b, c = ro + 2 - (2 * di + rp), co + 2 - (2 * dj + cp)
                            if 0 <= b < 3 and 0 <= c < 3:
                                for a in range(3):
                                    for ch in range(3):
                                        tap = ((a * 3 + b) * 3 + c) * 3 + ch
                                        m[di, dj, rp, cp, tap, a * 24 + ro * 12 + co * 3 + ch] = 1
    return m.reshape(16, 81, 80)


BLOCKS = ((1, 1), (1, 2), (2, 1), (2, 2), None, (1, 0), None, (2, 0), (0, 1), (0, 2), None, (0, 0))


def kernel(
    pos, clip, left, right, up, sel_mid, sel_side, spread, w1, b1, w2, b2, wb, wx, place,
    x_out, g_out,
    ct, p2, mk, sl, hf_a, hf_b, h6_a, h6_b, dacc, sdf, d4, dt, hdf_a, hdf_b, hd4_a, hd4_b, hds, yt, xs, tp, tpt,
    thf_a, thf_b, th6_a, th6_b, oacc, gacc, gf, strips, upf,
):
    r0, c0, rows, cols = pos[0], pos[1], pos[2], pos[3]

    def inside(r, c):
        return (r >= 0) & (r < rows) & (c >= 0) & (c < cols)

    sub = lax.broadcasted_iota(jnp.int32, (S, 256), 0)
    lane = lax.broadcasted_iota(jnp.int32, (S, 256), 1)
    for q in range(22):
        r = r0 + 2 * (q - 3) + (lane >> 7)
        c = c0 + 2 * (sub - 3) + ((lane >> 6) & 1)
        mk[q * S : (q + 1) * S, :] = jnp.where(inside(r, c), 1.0, 0.0)

    p2[0] = jnp.zeros(p2.shape[1:], F32)
    p2[T + 1] = jnp.zeros(p2.shape[1:], F32)
    yt[T + 2] = jnp.zeros(yt.shape[1:], F32)
    tp[...] = jnp.zeros(tp.shape, BF16)
    tpt[0] = jnp.zeros(tpt.shape[1:], BF16)
    tpt[T + 1] = jnp.zeros(tpt.shape[1:], BF16)
    oacc[...] = jnp.zeros(oacc.shape, F32)
    gacc[...] = jnp.zeros(gacc.shape, F32)
    sdf[480:496, :] = jnp.zeros((16, 128), F32)
    gf[...] = jnp.zeros(gf.shape, F32)
    upf[...] = jnp.zeros(upf.shape, F32)
    strips[0] = jnp.where(c0 > 0, left[...].astype(F32), 0.0)
    strips[1] = jnp.where(c0 + 32 < cols, right[...].astype(F32), 0.0)
    h6_b[...] = jnp.zeros(h6_b.shape, BF16)
    hd4_b[...] = jnp.zeros(hd4_b.shape, BF16)
    hds[0] = jnp.zeros(hds.shape[1:], BF16)
    th6_b[...] = jnp.zeros(th6_b.shape, BF16)

    @pl.loop(0, T, unroll=True)
    def _(t):
        middle = jnp.concatenate([clip[0, t], clip[1, t], clip[2, t]], axis=0)
        edges = jnp.concatenate(
            [
                jnp.concatenate(
                    [strips[k, pl.ds(pl.multiple_of((ch * T + t) * 8, 8), 8), 0:48] for ch in range(3)], axis=1
                )
                for k in range(2)
            ],
            axis=0,
        ).astype(BF16)
        turned = dot_nt(sel_mid[...], middle) + dot(sel_side[...], edges)
        at = pl.ds(pl.multiple_of(t * S, 8), S)
        for d in range(4):
            ct[d, at, :] = turned[d * S : (d + 1) * S]

    for n in range(0, 11, 2):
        width = min(2, 11 - n) * 128
        part = jnp.zeros((T * S, width), F32)
        for d in range(4):
            part += dot(ct[d].astype(BF16), spread[d, :, n * 128 : n * 128 + width])
        for k in range(width // 128):
            q = n + k
            p2[1 : T + 1, q * S : (q + 1) * S, :] = part[:, k * 128 : (k + 1) * 128].reshape(T, S, 128)

    for p in range(TO + 1):
        dacc[p] = jnp.broadcast_to(b2[...], (480, 128))

    def hidden(t, hf, h6):
        lhs = jnp.concatenate([p2[t], p2[t + 1], p2[t + 2]], axis=1).astype(BF16)
        pre = dot(lhs, w1[...]) + jnp.concatenate([b1[...]] * 8, axis=1)
        slope = jnp.where(pre > 0, 1.0, LEAK)
        for q in range(11):
            for e in range(2):
                to = slice((2 * q + e) * S, (2 * q + e + 1) * S)
                of = (slice(q * S, (q + 1) * S), slice(e * 256, (e + 1) * 256))
                masked = slope[of] * mk[to, :]
                sl[t, to, :] = masked
                hf[to, :] = pre[of] * masked
        h6[:, 0:256] = hf[25:505, :].astype(BF16)
        h6[:, 256:512] = hf[24:504, :].astype(BF16)
        h6[:, 512:640] = hf[1:481, 128:256].astype(BF16)
        h6[:, 640:768] = hf[0:480, 128:256].astype(BF16)

    def odd_second(p):
        both = dot(h6_b[...], w2[:, 0:256])
        dacc[p + 1] += both[:, 0:128]
        dacc[p + 2] += both[:, 128:256]

    def even_second(p):
        dacc[p + 1] += dot(h6_a[...], w2[:, 256:384])

    @pl.loop(0, TO - 1, unroll=True)
    def _(p):
        hidden(2 * p, hf_a, h6_a)
        odd_second(p - 1)
        hidden(2 * p + 1, hf_b, h6_b)
        even_second(p)

    hidden(2 * TO - 2, hf_a, h6_a)
    odd_second(TO - 2)
    even_second(TO - 1)

    at384 = lax.broadcasted_iota(jnp.int32, (384, 128), 0)
    core = jnp.where(at384 % S < 16, 1.0, 0.0)

    for p in range(TO):
        slope = jnp.where(dacc[p + 1] > 0, 1.0, LEAK)
        for q in range(20):
            upf[q * S + 2 : q * S + 18, :] = up[p, q].astype(F32)
        for s in range(2):
            of = slice(408 + (p * 2 + s) * 20, 428 + (p * 2 + s) * 20)
            upf[pl.ds(s, 20, stride=S), :] = strips[0, of, :]
            upf[pl.ds(18 + s, 20, stride=S), :] = strips[1, of, :]
        sdf[0:480, :] = upf[...] * slope
        d4[p, :, 0:128] = sdf[0:464, :].astype(BF16)
        d4[p, :, 128:256] = sdf[1:465, :].astype(BF16)
        d4[p, :, 256:384] = sdf[24:488, :].astype(BF16)
        d4[p, :, 384:512] = sdf[25:489, :].astype(BF16)
        dt[p] = jnp.transpose(sdf[50:434, :] * core).astype(BF16)

    def delta(t, back, hdf, hd4):
        hdf[...] = back * sl[t, 25:489, :]
        hds[t + 1] = hdf[25:457, :].astype(BF16)
        hd4[:, 0:256] = hdf[0:432, :].astype(BF16)
        hd4[:, 256:512] = hdf[1:433, :].astype(BF16)
        hd4[:, 512:768] = hdf[24:456, :].astype(BF16)

    def products(t, hd4):
        yt[t + 2, :, 0:432] = dot_nt(wx[:, 0:768], hd4[...]) + dot_nt(wx[:, 768:1024], hds[t + 1])

    @pl.loop(0, TO - 1, unroll=True)
    def _(p):
        delta(2 * p, dot(d4[p], wb[0:512, :]), hdf_a, hd4_a)
        products(2 * p - 1, hd4_b)
        lhs = jnp.concatenate([d4[p], d4[p + 1]], axis=1)
        delta(2 * p + 1, dot(lhs, wb[512:1536, :]), hdf_b, hd4_b)
        products(2 * p, hd4_a)

    delta(2 * TO - 2, dot(d4[TO - 1], wb[0:512, :]), hdf_a, hd4_a)
    products(2 * TO - 3, hd4_b)
    products(2 * TO - 2, hd4_a)

    index = lax.broadcasted_iota(jnp.int32, (S, 512), 0)
    cell = lax.broadcasted_iota(jnp.int32, (S, 512), 1)
    second_row = index >= 12
    in_row = jnp.where(second_row, index - 12, index)
    r = r0 + 2 * (cell // S) - 3 + jnp.where(second_row, 1, 0)
    c = c0 + 2 * (cell % S) - 3 + jnp.where(in_row >= 3, 1, 0)
    live = inside(r, c) & (in_row < 6) & (cell < 432)
    cell = lax.broadcasted_iota(jnp.int32, (48, 416), 1)
    core_first = (cell % S >= 1) & (cell % S <= 16) & (cell >= S) & (cell < 17 * S)
    cell = lax.broadcasted_iota(jnp.int32, (S, 512), 1)

    @pl.loop(0, T, unroll=True)
    def _(t):
        x = yt[t + 3, 0:24, :] + yt[t + 2, 24:48, :] + yt[t + 1, 48:72, :]
        x = jnp.where(cell < 432, x, 0.0)
        at = pl.ds(pl.multiple_of(t * 48, 16), 48)
        for co in range(2):
            here = x if co == 0 else pltpu.roll(x, 21, 0)
            high = here.astype(BF16).astype(F32)
            xs[at, co * 512 : (co + 1) * 512] = jnp.concatenate([high, here - high], axis=0).astype(BF16)
        m = jnp.where(live, x, 0.0)
        upper = m + pltpu.roll(pltpu.roll(m, 511, 1), 6, 0)
        lower = pltpu.roll(m, 488, 1) + pltpu.roll(pltpu.roll(m, 487, 1), 6, 0)
        wide = jnp.concatenate([upper, lower], axis=0)
        tpt[t + 1] = jnp.where(core_first, wide[:, 0:416], 0.0).astype(BF16)
        tp[t + 1, :, 0:48] = jnp.transpose(wide)[0:416].astype(BF16)

    for n in range(T):
        placed = dot(xs[n * 48 : (n + 1) * 48, :], place[...])
        placed = placed[0:24] + placed[24:48]
        for p in range(18):
            for ro in range(2):
                row = 2 * p - 3 + ro
                if 0 <= row < 32:
                    for ch in range(3):
                        k = ro * 12 + ch
                        x_out[ch, n, row : row + 1, :] = placed[k : k + 1, p * 32 : p * 32 + 32]

    def tangents(t, thf, th6):
        lhs = jnp.concatenate([tp[t], tp[t + 1], tp[t + 2]], axis=1)
        thf[...] = dot(lhs, w1[:, 0:256]) * sl[t, 50:466, :]
        th6[:, 0:256] = thf[25:409, :].astype(BF16)
        th6[:, 256:512] = thf[24:408, :].astype(BF16)
        th6[:, 512:640] = thf[1:385, 128:256].astype(BF16)
        th6[:, 640:768] = thf[0:384, 128:256].astype(BF16)
        turned = jnp.concatenate([tpt[t], tpt[t + 1], tpt[t + 2]], axis=0)
        gacc[...] += dot(turned, hds[t + 1, 0:416, :])

    def odd_terms(p):
        oacc[256:384, :] += dot(dt[jnp.maximum(p, 0)], th6_b[...])
        oacc[0:128, :] += dot(dt[p + 1], th6_b[...])

    def even_terms(p):
        oacc[128:256, :] += dot(dt[p], th6_a[...])

    @pl.loop(0, TO - 1, unroll=True)
    def _(p):
        tangents(2 * p, thf_a, th6_a)
        odd_terms(p - 1)
        tangents(2 * p + 1, thf_b, th6_b)
        even_terms(p)

    tangents(2 * TO - 2, thf_a, th6_a)
    odd_terms(TO - 2)
    even_terms(TO - 1)

    for a in range(3):
        for b in range(3):
            total = jnp.zeros((9, 64), F32)
            for rp in range(2):
                for cp in range(2):
                    start = a * 48 + (b + rp) * 12 + cp * 3
                    part = (rp * 2 + cp) * 64
                    total += gacc[start : start + 9, part : part + 64]
            gf[a * 27 + b * 9 : a * 27 + b * 9 + 9, :] = total

    left_half = lax.broadcasted_iota(jnp.int32, (8, 128), 1) < 64
    ends = jnp.concatenate([gf[24:56, :], gf[53:85, :]], axis=1)
    ends = jnp.concatenate([ends, jnp.zeros((8, 128), F32)], axis=0)
    start = jnp.concatenate([gf[0:24, :], jnp.zeros((24, 64), F32)], axis=1)
    for w in range(16):
        tiles = [[oacc[a * 128 + w * 8 : a * 128 + w * 8 + 8, k * 128 : k * 128 + 128] for a in range(3)] for k in range(6)]
        mixed = [jnp.where(left_half, pltpu.roll(tiles[2][a], 64, 1), tiles[3][a]) for a in range(3)]
        last = [jnp.where(left_half, start[a * 8 : a * 8 + 8], tiles[5][a]) for a in range(3)]
        g_out[w] = jnp.concatenate(tiles[0] + tiles[1] + mixed + tiles[4] + last + [ends], axis=0).astype(BF16)


TAPS = ((1, 1), (1, 2), (2, 1), (2, 2), (1, 0), (2, 0), (0, 1), (0, 2), None, (0, 0))


def run_kernel(*args):
    vm = lambda shape, kind=F32: pltpu.VMEM(shape, kind)
    vmem = pl.BlockSpec(memory_space=pltpu.VMEM)
    return pl.pallas_call(
        kernel,
        out_shape=(
            jax.ShapeDtypeStruct((3, T, 32, 32), F32),
            jax.ShapeDtypeStruct((16, 160, 128), BF16),
        ),
        in_specs=[pl.BlockSpec(memory_space=pltpu.SMEM)] + [vmem] * 14,
        out_specs=(vmem, vmem),
        scratch_shapes=[
            vm((4, T * S, 144)),
            vm((T + 2, 264, 128)),
            vm((528, 256)),
            vm((T, 528, 256)),
            vm((528, 256)),
            vm((528, 256)),
            vm((480, 768), BF16),
            vm((480, 768), BF16),
            vm((TO + 1, 480, 128)),
            vm((496, 128)),
            vm((TO, 464, 512), BF16),
            vm((TO, 128, 384), BF16),
            vm((464, 256)),
            vm((464, 256)),
            vm((432, 768), BF16),
            vm((432, 768), BF16),
            vm((T + 1, 432, 256), BF16),
            vm((T + 3, 80, 512)),
            vm((T * 48, 1024), BF16),
            vm((T + 2, 416, 128), BF16),
            vm((T + 2, 48, 416), BF16),
            vm((416, 256)),
            vm((416, 256)),
            vm((384, 768), BF16),
            vm((384, 768), BF16),
            vm((384, 768)),
            vm((144, 256)),
            vm((96, 64)),
            vm((2, 768, 128)),
            vm((480, 128)),
        ],
        compiler_params=pltpu.CompilerParams(vmem_limit_bytes=60 * 1024 * 1024),
        cost_estimate=pl.CostEstimate(flops=10**10, bytes_accessed=2 * 10**7, transcendentals=0),
    )(*args)


def swapped(to_next, to_prev, axis):
    size = lax.axis_size(axis)
    ring = [(i, (i + 1) % size) for i in range(size)]
    return lax.ppermute(to_next, axis, ring), lax.ppermute(to_prev, axis, [(j, i) for i, j in ring])


def packed(clip_part, up_part):
    flat = clip_part.reshape(408, clip_part.shape[3])
    flat = jnp.pad(flat, ((0, 0), (0, 128 - flat.shape[1])))
    return jnp.concatenate([flat, up_part.reshape(-1, 128)], axis=0)


def body(clip, w_first, b_first, w_second, b_second, upstream):
    rows = clip.shape[2] * lax.axis_size("ha")
    cols = clip.shape[3] * lax.axis_size("wa")
    ha, wa = lax.axis_index("ha"), lax.axis_index("wa")
    pos = jnp.stack([ha * 32, wa * 32, jnp.int32(rows), jnp.int32(cols)]).astype(jnp.int32)

    above, below = swapped(
        packed(clip[:, :, 24:32], upstream[:, 14:16]), packed(clip[:, :, 0:8], upstream[:, 0:2]), "ha"
    )
    above, below, w_second = lax.optimization_barrier((above, below, w_second))
    above = jnp.where(ha > 0, above, jnp.zeros_like(above))
    below = jnp.where(ha < lax.axis_size("ha") - 1, below, jnp.zeros_like(below))
    clip_part = lambda v, width: v[:408, :width].reshape(3, T, 8, width)
    clip_rows = jnp.concatenate([clip_part(above, 32), clip, clip_part(below, 32)], axis=2)
    up_part = lambda v: v[408:].reshape(TO, 2, 16, 128)
    up_rows = jnp.concatenate([up_part(above), upstream, up_part(below)], axis=1)
    left, right = swapped(
        packed(jnp.swapaxes(clip_rows[:, :, :, 24:32], 2, 3), jnp.swapaxes(up_rows[:, :, 14:16], 1, 2)),
        packed(jnp.swapaxes(clip_rows[:, :, :, 0:8], 2, 3), jnp.swapaxes(up_rows[:, :, 0:2], 1, 2)),
        "wa",
    )

    w_flat = w_first.reshape(81, 64)
    diagonal = jnp.concatenate(
        [jnp.pad(w_flat, ((0, 0), (64 * k, 192 - 64 * k))) for k in range(4)], axis=0
    )
    forward_pick = jnp.asarray(first_forward(), BF16)
    w1 = jnp.concatenate(
        [dot(forward_pick[:, e], diagonal).astype(BF16) for e in range(2)], axis=1
    )
    wx = jnp.einsum(
        "ko,bkl->lbo", w_flat, jnp.asarray(first_backward(), BF16), preferred_element_type=F32
    )
    wx = wx.astype(BF16).reshape(80, 1024)
    nothing = jnp.zeros((64, 128), BF16)
    w2 = jnp.concatenate(
        [
            jnp.concatenate(
                [nothing if k is None else w_second[a, k[0], k[1]] for k in BLOCKS], axis=0
            )
            for a in (2, 0, 1)
        ],
        axis=1,
    )
    turned = jnp.swapaxes(w_second, 3, 4)
    blank = jnp.zeros((128, 64), BF16)
    pieces = []
    for a in (1, 2, 0):
        for dq in range(2):
            for ds in range(2):
                line = []
                for rp in range(2):
                    for cp in range(2):
                        b, c = rp + 1 - 2 * dq, cp + 1 - 2 * ds
                        line.append(turned[a, b, c] if b >= 0 and c >= 0 else blank)
                pieces.append(jnp.concatenate(line, axis=1))
    wb = jnp.concatenate(pieces, axis=0)

    middle, first8, last8 = pick_columns()
    input_grad, terms = run_kernel(
        pos,
        clip_rows,
        left,
        right,
        up_rows,
        jnp.asarray(middle, BF16),
        jnp.asarray(np.concatenate([first8, last8], axis=1), BF16),
        jnp.asarray(spread_rows(), BF16),
        w1,
        b_first[None],
        w2,
        b_second[None],
        wb,
        wx,
        jnp.asarray(place_columns(), BF16),
    )

    scale = 1.0 / (T * rows * cols)
    part = lax.all_to_all(terms, "wa", 0, 0, tiled=True)
    part = part.astype(F32).sum(0)
    step = 1
    while step < lax.axis_size("ha"):
        part = part + lax.ppermute(part, "ha", [(i, i ^ step) for i in range(lax.axis_size("ha"))])
        step *= 2
    part = part * scale
    lane = lax.broadcasted_iota(jnp.int32, (128, 16), 0)
    mine = lax.broadcasted_iota(jnp.int32, (128, 16), 1)
    pick = (lane == (mine // 8) * 64 + ha * 8 + mine % 8).astype(F32)
    second = jnp.dot(part[0:120], pick, precision=lax.Precision.HIGHEST, preferred_element_type=F32)
    second = second.reshape(5, 3, 8, 2, 8)
    keep = [TAPS.index((b, c)) for b in range(3) for c in range(3)]
    second = second.transpose(0, 3, 1, 4, 2).reshape(10, 3, 8, 8)
    grad_second = jnp.stack([second[k] for k in keep], axis=1).reshape(3, 3, 3, 8, 8)
    first = part[96:160]
    grad_first = jnp.concatenate([first[0:24, 0:64], first[24:53, 0:64], first[24:53, 64:128]], axis=0)
    grad_first = grad_first[:81].reshape(3, 3, 3, 3, 64)
    return (input_grad, grad_first, grad_second)


def solution(mesh):
    placed = (P(None, None, "ha", "wa"), P(), P(), P(), P(), P(None, "ha", "wa", None))
    return jax.shard_map(
        body,
        mesh=mesh,
        in_specs=placed,
        out_specs=(P(None, None, "ha", "wa"), P(), P(None, None, None, "ha", "wa")),
        check_vma=False,
    )
```

```python
import numpy as np
import jax
import jax.numpy as jnp
from jax import lax
from jax.experimental import pallas as pl
from jax.experimental.pallas import tpu as pltpu
from jax.sharding import PartitionSpec as P

LEAK = 0.2
T = 17
TO = 9
S = 24
F32 = jnp.float32
BF16 = jnp.bfloat16


def dot(a, b):
    return jnp.dot(a, b, preferred_element_type=F32)


def dot_nt(a, b):
    return lax.dot_general(a, b, (((1,), (1,)), ((), ())), preferred_element_type=F32)


def pick_columns():
    m = np.zeros((4, S, 48), np.float32)
    for d in range(4):
        for s in range(22):
            m[d, s, 2 * s + d + 1] = 1
    m = m.reshape(4 * S, 48)
    return m[:, 8:40], m[:, :8], m[:, 40:]


def place_columns():
    m = np.zeros((2, 512, 18, 32), np.float32)
    for p in range(18):
        for s in range(18):
            for co in range(2):
                if 0 <= 2 * s - 3 + co < 32:
                    m[co, p * S + s, p, 2 * s - 3 + co] = 1
    return m.reshape(1024, 576)


def spread_rows():
    m = np.zeros((4, 144, 11, 2, 64), np.float32)
    for d in range(4):
        for q in range(22):
            for k in range(4):
                for ch in range(3):
                    if 2 * q + k + 1 < 48:
                        m[d, ch * 48 + 2 * q + k + 1, q // 2, q % 2, k * 12 + d * 3 + ch] = 1
    return m.reshape(4, 144, 11 * 128)


def first_forward():
    m = np.zeros((3, 128, 2, 4, 81), np.float32)
    for a in range(3):
        for k in range(4):
            for d in range(4):
                for ch in range(3):
                    for rp in range(2):
                        for cp in range(2):
                            b, c = k - rp, d - cp
                            if 0 <= b < 3 and 0 <= c < 3:
                                tap = ((a * 3 + b) * 3 + c) * 3 + ch
                                lane = k * 12 + d * 3 + ch
                                m[a, lane, 0, rp * 2 + cp, tap] = 1
                                m[a, 64 + lane, 1, rp * 2 + cp, tap] = 1
    return m.reshape(384, 2, 4 * 81)


def first_backward():
    m = np.zeros((2, 2, 2, 2, 81, 80), np.float32)
    for di in range(2):
        for dj in range(2):
            for rp in range(2):
                for cp in range(2):
                    for ro in range(2):
                        for co in range(2):
                            b, c = ro + 2 - (2 * di + rp), co + 2 - (2 * dj + cp)
                            if 0 <= b < 3 and 0 <= c < 3:
                                for a in range(3):
                                    for ch in range(3):
                                        tap = ((a * 3 + b) * 3 + c) * 3 + ch
                                        m[di, dj, rp, cp, tap, a * 24 + ro * 12 + co * 3 + ch] = 1
    return m.reshape(16, 81, 80)


BLOCKS = ((1, 1), (1, 2), (2, 1), (2, 2), None, (1, 0), None, (2, 0), (0, 1), (0, 2), None, (0, 0))


def kernel(
    pos, clip, left, right, up, sel_mid, sel_side, spread, w1, b1, w_second, b2, wx, place,
    x_out, g_out,
    ct, p2, mk, sl, hf_a, hf_b, h6_a, h6_b, dacc, sdf, d4, dt, hdf_a, hdf_b, hd4_a, hd4_b, hds, yt, xs, tp, tpt,
    thf_a, thf_b, th6_a, th6_b, oacc, gacc, gf, strips, upf, w2, wb,
):
    r0, c0, rows, cols = pos[0], pos[1], pos[2], pos[3]

    def inside(r, c):
        return (r >= 0) & (r < rows) & (c >= 0) & (c < cols)

    sub = lax.broadcasted_iota(jnp.int32, (S, 256), 0)
    lane = lax.broadcasted_iota(jnp.int32, (S, 256), 1)
    for q in range(22):
        r = r0 + 2 * (q - 3) + (lane >> 7)
        c = c0 + 2 * (sub - 3) + ((lane >> 6) & 1)
        mk[q * S : (q + 1) * S, :] = jnp.where(inside(r, c), 1.0, 0.0)

    p2[0] = jnp.zeros(p2.shape[1:], F32)
    p2[T + 1] = jnp.zeros(p2.shape[1:], F32)
    yt[T + 2] = jnp.zeros(yt.shape[1:], F32)
    tp[...] = jnp.zeros(tp.shape, BF16)
    tpt[0] = jnp.zeros(tpt.shape[1:], BF16)
    tpt[T + 1] = jnp.zeros(tpt.shape[1:], BF16)
    oacc[...] = jnp.zeros(oacc.shape, F32)
    gacc[...] = jnp.zeros(gacc.shape, F32)
    sdf[480:496, :] = jnp.zeros((16, 128), F32)
    gf[...] = jnp.zeros(gf.shape, F32)
    upf[...] = jnp.zeros(upf.shape, F32)

    for n, a in enumerate((2, 0, 1)):
        for k, tap in enumerate(BLOCKS):
            block = jnp.zeros((64, 128), BF16) if tap is None else w_second[a * 9 + tap[0] * 3 + tap[1]]
            w2[k * 64 : (k + 1) * 64, n * 128 : (n + 1) * 128] = block
    for n, a in enumerate((1, 2, 0)):
        for dq in range(2):
            for ds in range(2):
                for rp in range(2):
                    b = rp + 1 - 2 * dq
                    pair = jnp.zeros((128, 128), F32)
                    if b >= 0:
                        taps = [w_second[a * 9 + b * 3 + c].astype(F32) for c in ((0,) if ds else (1, 2))]
                        pair = jnp.concatenate([jnp.zeros((64, 128), F32)] * ds + taps, axis=0)
                    to = (n * 4 + dq * 2 + ds) * 128
                    wb[to : to + 128, rp * 128 : (rp + 1) * 128] = jnp.transpose(pair).astype(BF16)

    strips[0] = jnp.where(c0 > 0, left[...].astype(F32), 0.0)
    strips[1] = jnp.where(c0 + 32 < cols, right[...].astype(F32), 0.0)
    h6_b[...] = jnp.zeros(h6_b.shape, BF16)
    hd4_b[...] = jnp.zeros(hd4_b.shape, BF16)
    hds[0] = jnp.zeros(hds.shape[1:], BF16)
    th6_b[...] = jnp.zeros(th6_b.shape, BF16)

    @pl.loop(0, T, unroll=True)
    def _(t):
        middle = jnp.concatenate([clip[0, t], clip[1, t], clip[2, t]], axis=0)
        edges = jnp.concatenate(
            [
                jnp.concatenate(
                    [strips[k, pl.ds(pl.multiple_of((ch * T + t) * 8, 8), 8), 0:48] for ch in range(3)], axis=1
                )
                for k in range(2)
            ],
            axis=0,
        ).astype(BF16)
        turned = dot_nt(sel_mid[...], middle) + dot(sel_side[...], edges)
        at = pl.ds(pl.multiple_of(t * S, 8), S)
        for d in range(4):
            ct[d, at, :] = turned[d * S : (d + 1) * S]

    for n in range(0, 11, 2):
        width = min(2, 11 - n) * 128
        part = jnp.zeros((T * S, width), F32)
        for d in range(4):
            part += dot(ct[d].astype(BF16), spread[d, :, n * 128 : n * 128 + width])
        for k in range(width // 128):
            q = n + k
            p2[1 : T + 1, q * S : (q + 1) * S, :] = part[:, k * 128 : (k + 1) * 128].reshape(T, S, 128)

    for p in range(TO + 1):
        dacc[p] = jnp.broadcast_to(b2[...], (480, 128))

    def hidden(t, hf, h6):
        lhs = jnp.concatenate([p2[t], p2[t + 1], p2[t + 2]], axis=1).astype(BF16)
        pre = dot(lhs, w1[...]) + jnp.concatenate([b1[...]] * 8, axis=1)
        slope = jnp.where(pre > 0, 1.0, LEAK)
        for q in range(11):
            for e in range(2):
                to = slice((2 * q + e) * S, (2 * q + e + 1) * S)
                of = (slice(q * S, (q + 1) * S), slice(e * 256, (e + 1) * 256))
                masked = slope[of] * mk[to, :]
                sl[t, to, :] = masked
                hf[to, :] = pre[of] * masked
        h6[:, 0:256] = hf[25:505, :].astype(BF16)
        h6[:, 256:512] = hf[24:504, :].astype(BF16)
        h6[:, 512:640] = hf[1:481, 128:256].astype(BF16)
        h6[:, 640:768] = hf[0:480, 128:256].astype(BF16)

    def odd_second(p):
        both = dot(h6_b[...], w2[:, 0:256])
        dacc[p + 1] += both[:, 0:128]
        dacc[p + 2] += both[:, 128:256]

    def even_second(p):
        dacc[p + 1] += dot(h6_a[...], w2[:, 256:384])

    @pl.loop(0, TO - 1, unroll=True)
    def _(p):
        hidden(2 * p, hf_a, h6_a)
        odd_second(p - 1)
        hidden(2 * p + 1, hf_b, h6_b)
        even_second(p)

    hidden(2 * TO - 2, hf_a, h6_a)
    odd_second(TO - 2)
    even_second(TO - 1)

    at384 = lax.broadcasted_iota(jnp.int32, (384, 128), 0)
    core = jnp.where(at384 % S < 16, 1.0, 0.0)

    for p in range(TO):
        slope = jnp.where(dacc[p + 1] > 0, 1.0, LEAK)
        for q in range(20):
            upf[q * S + 2 : q * S + 18, :] = up[p, q].astype(F32)
        for s in range(2):
            of = slice(408 + (p * 2 + s) * 20, 428 + (p * 2 + s) * 20)
            upf[pl.ds(s, 20, stride=S), :] = strips[0, of, :]
            upf[pl.ds(18 + s, 20, stride=S), :] = strips[1, of, :]
        sdf[0:480, :] = upf[...] * slope
        d4[p, :, 0:128] = sdf[0:464, :].astype(BF16)
        d4[p, :, 128:256] = sdf[1:465, :].astype(BF16)
        d4[p, :, 256:384] = sdf[24:488, :].astype(BF16)
        d4[p, :, 384:512] = sdf[25:489, :].astype(BF16)
        dt[p] = jnp.transpose(sdf[50:434, :] * core).astype(BF16)

    def delta(t, back, hdf, hd4):
        hdf[...] = back * sl[t, 25:489, :]
        hds[t + 1] = hdf[25:457, :].astype(BF16)
        hd4[:, 0:256] = hdf[0:432, :].astype(BF16)
        hd4[:, 256:512] = hdf[1:433, :].astype(BF16)
        hd4[:, 512:768] = hdf[24:456, :].astype(BF16)

    def products(t, hd4):
        yt[t + 2, :, 0:432] = dot_nt(wx[:, 0:768], hd4[...]) + dot_nt(wx[:, 768:1024], hds[t + 1])

    @pl.loop(0, TO - 1, unroll=True)
    def _(p):
        delta(2 * p, dot(d4[p], wb[0:512, :]), hdf_a, hd4_a)
        products(2 * p - 1, hd4_b)
        lhs = jnp.concatenate([d4[p], d4[p + 1]], axis=1)
        delta(2 * p + 1, dot(lhs, wb[512:1536, :]), hdf_b, hd4_b)
        products(2 * p, hd4_a)

    delta(2 * TO - 2, dot(d4[TO - 1], wb[0:512, :]), hdf_a, hd4_a)
    products(2 * TO - 3, hd4_b)
    products(2 * TO - 2, hd4_a)

    index = lax.broadcasted_iota(jnp.int32, (S, 512), 0)
    cell = lax.broadcasted_iota(jnp.int32, (S, 512), 1)
    second_row = index >= 12
    in_row = jnp.where(second_row, index - 12, index)
    r = r0 + 2 * (cell // S) - 3 + jnp.where(second_row, 1, 0)
    c = c0 + 2 * (cell % S) - 3 + jnp.where(in_row >= 3, 1, 0)
    live = inside(r, c) & (in_row < 6) & (cell < 432)
    cell = lax.broadcasted_iota(jnp.int32, (48, 416), 1)
    core_first = (cell % S >= 1) & (cell % S <= 16) & (cell >= S) & (cell < 17 * S)
    cell = lax.broadcasted_iota(jnp.int32, (S, 512), 1)

    @pl.loop(0, T, unroll=True)
    def _(t):
        x = yt[t + 3, 0:24, :] + yt[t + 2, 24:48, :] + yt[t + 1, 48:72, :]
        x = jnp.where(cell < 432, x, 0.0)
        at = pl.ds(pl.multiple_of(t * 48, 16), 48)
        for co in range(2):
            here = x if co == 0 else pltpu.roll(x, 21, 0)
            high = here.astype(BF16).astype(F32)
            xs[at, co * 512 : (co + 1) * 512] = jnp.concatenate([high, here - high], axis=0).astype(BF16)
        m = jnp.where(live, x, 0.0)
        upper = m + pltpu.roll(pltpu.roll(m, 511, 1), 6, 0)
        lower = pltpu.roll(m, 488, 1) + pltpu.roll(pltpu.roll(m, 487, 1), 6, 0)
        wide = jnp.concatenate([upper, lower], axis=0)
        tpt[t + 1] = jnp.where(core_first, wide[:, 0:416], 0.0).astype(BF16)
        tp[t + 1, :, 0:48] = jnp.transpose(wide)[0:416].astype(BF16)

    for first in range(0, T, 6):
        frames = range(first, min(first + 6, T))
        group = dot(xs[first * 48 : (frames[-1] + 1) * 48, :], place[...])
        for n in frames:
            at = (n - first) * 48
            placed = group[at : at + 24] + group[at + 24 : at + 48]
            for p in range(18):
                for ro in range(2):
                    row = 2 * p - 3 + ro
                    if 0 <= row < 32:
                        for ch in range(3):
                            k = ro * 12 + ch
                            x_out[ch, n, row : row + 1, :] = placed[k : k + 1, p * 32 : p * 32 + 32]

    def tangents(t, thf, th6):
        lhs = jnp.concatenate([tp[t], tp[t + 1], tp[t + 2]], axis=1)
        thf[...] = dot(lhs, w1[:, 0:256]) * sl[t, 50:466, :]
        th6[:, 0:256] = thf[25:409, :].astype(BF16)
        th6[:, 256:512] = thf[24:408, :].astype(BF16)
        th6[:, 512:640] = thf[1:385, 128:256].astype(BF16)
        th6[:, 640:768] = thf[0:384, 128:256].astype(BF16)
        turned = jnp.concatenate([tpt[t], tpt[t + 1], tpt[t + 2]], axis=0)
        gacc[...] += dot(turned, hds[t + 1, 0:416, :])

    def odd_terms(p):
        both = dot(dt[pl.ds(jnp.maximum(p, 0), 2)].reshape(256, 384), th6_b[...])
        oacc[256:384, :] += both[0:128]
        oacc[0:128, :] += both[128:256]

    def even_terms(p):
        oacc[128:256, :] += dot(dt[p], th6_a[...])

    @pl.loop(0, TO - 1, unroll=True)
    def _(p):
        tangents(2 * p, thf_a, th6_a)
        odd_terms(p - 1)
        tangents(2 * p + 1, thf_b, th6_b)
        even_terms(p)

    tangents(2 * TO - 2, thf_a, th6_a)
    odd_terms(TO - 2)
    even_terms(TO - 1)

    for a in range(3):
        for b in range(3):
            total = jnp.zeros((9, 64), F32)
            for rp in range(2):
                for cp in range(2):
                    start = a * 48 + (b + rp) * 12 + cp * 3
                    part = (rp * 2 + cp) * 64
                    total += gacc[start : start + 9, part : part + 64]
            gf[a * 27 + b * 9 : a * 27 + b * 9 + 9, :] = total

    left_half = lax.broadcasted_iota(jnp.int32, (8, 128), 1) < 64
    ends = jnp.concatenate([gf[24:56, :], gf[53:85, :]], axis=1)
    ends = jnp.concatenate([ends, jnp.zeros((8, 128), F32)], axis=0)
    start = jnp.concatenate([gf[0:24, :], jnp.zeros((24, 64), F32)], axis=1)
    for w in range(16):
        tiles = [[oacc[a * 128 + w * 8 : a * 128 + w * 8 + 8, k * 128 : k * 128 + 128] for a in range(3)] for k in range(6)]
        mixed = [jnp.where(left_half, pltpu.roll(tiles[2][a], 64, 1), tiles[3][a]) for a in range(3)]
        last = [jnp.where(left_half, start[a * 8 : a * 8 + 8], tiles[5][a]) for a in range(3)]
        g_out[w] = jnp.concatenate(tiles[0] + tiles[1] + mixed + tiles[4] + last + [ends], axis=0).astype(BF16)


TAPS = ((1, 1), (1, 2), (2, 1), (2, 2), (1, 0), (2, 0), (0, 1), (0, 2), None, (0, 0))


def run_kernel(*args):
    vm = lambda shape, kind=F32: pltpu.VMEM(shape, kind)
    vmem = pl.BlockSpec(memory_space=pltpu.VMEM)
    return pl.pallas_call(
        kernel,
        out_shape=(
            jax.ShapeDtypeStruct((3, T, 32, 32), F32),
            jax.ShapeDtypeStruct((16, 160, 128), BF16),
        ),
        in_specs=[pl.BlockSpec(memory_space=pltpu.SMEM)] + [vmem] * 13,
        out_specs=(vmem, vmem),
        scratch_shapes=[
            vm((4, T * S, 144)),
            vm((T + 2, 264, 128)),
            vm((528, 256)),
            vm((T, 528, 256)),
            vm((528, 256)),
            vm((528, 256)),
            vm((480, 768), BF16),
            vm((480, 768), BF16),
            vm((TO + 1, 480, 128)),
            vm((496, 128)),
            vm((TO, 464, 512), BF16),
            vm((TO, 128, 384), BF16),
            vm((464, 256)),
            vm((464, 256)),
            vm((432, 768), BF16),
            vm((432, 768), BF16),
            vm((T + 1, 432, 256), BF16),
            vm((T + 3, 80, 512)),
            vm((T * 48, 1024), BF16),
            vm((T + 2, 416, 128), BF16),
            vm((T + 2, 48, 416), BF16),
            vm((416, 256)),
            vm((416, 256)),
            vm((384, 768), BF16),
            vm((384, 768), BF16),
            vm((384, 768)),
            vm((144, 256)),
            vm((96, 64)),
            vm((2, 768, 128)),
            vm((480, 128)),
            vm((768, 384), BF16),
            vm((1536, 256), BF16),
        ],
        compiler_params=pltpu.CompilerParams(vmem_limit_bytes=60 * 1024 * 1024),
        cost_estimate=pl.CostEstimate(flops=10**10, bytes_accessed=2 * 10**7, transcendentals=0),
    )(*args)


def swapped(to_next, to_prev, axis):
    size = lax.axis_size(axis)
    ring = [(i, (i + 1) % size) for i in range(size)]
    return lax.ppermute(to_next, axis, ring), lax.ppermute(to_prev, axis, [(j, i) for i, j in ring])


def packed(clip_part, up_part):
    flat = clip_part.reshape(408, clip_part.shape[3])
    flat = jnp.pad(flat, ((0, 0), (0, 128 - flat.shape[1])))
    return jnp.concatenate([flat, up_part.reshape(-1, 128)], axis=0)


def body(clip, w_first, b_first, w_second, b_second, upstream):
    rows = clip.shape[2] * lax.axis_size("ha")
    cols = clip.shape[3] * lax.axis_size("wa")
    ha, wa = lax.axis_index("ha"), lax.axis_index("wa")
    pos = jnp.stack([ha * 32, wa * 32, jnp.int32(rows), jnp.int32(cols)]).astype(jnp.int32)

    above, below = swapped(
        packed(clip[:, :, 24:32], upstream[:, 14:16]), packed(clip[:, :, 0:8], upstream[:, 0:2]), "ha"
    )
    above = jnp.where(ha > 0, above, jnp.zeros_like(above))
    below = jnp.where(ha < lax.axis_size("ha") - 1, below, jnp.zeros_like(below))
    clip_part = lambda v, width: v[:408, :width].reshape(3, T, 8, width)
    clip_rows = jnp.concatenate([clip_part(above, 32), clip, clip_part(below, 32)], axis=2)
    up_part = lambda v: v[408:].reshape(TO, 2, 16, 128)
    up_rows = jnp.concatenate([up_part(above), upstream, up_part(below)], axis=1)
    left, right = swapped(
        packed(jnp.swapaxes(clip_rows[:, :, :, 24:32], 2, 3), jnp.swapaxes(up_rows[:, :, 14:16], 1, 2)),
        packed(jnp.swapaxes(clip_rows[:, :, :, 0:8], 2, 3), jnp.swapaxes(up_rows[:, :, 0:2], 1, 2)),
        "wa",
    )

    w_flat = w_first.reshape(81, 64)
    diagonal = jnp.concatenate(
        [jnp.pad(w_flat, ((0, 0), (64 * k, 192 - 64 * k))) for k in range(4)], axis=0
    )
    forward_pick = jnp.asarray(first_forward(), BF16)
    w1 = jnp.concatenate(
        [dot(forward_pick[:, e], diagonal).astype(BF16) for e in range(2)], axis=1
    )
    wx = jnp.einsum(
        "ko,bkl->lbo", w_flat, jnp.asarray(first_backward(), BF16), preferred_element_type=F32
    )
    wx = wx.astype(BF16).reshape(80, 1024)
    middle, first8, last8 = pick_columns()
    input_grad, terms = run_kernel(
        pos,
        clip_rows,
        left,
        right,
        up_rows,
        jnp.asarray(middle, BF16),
        jnp.asarray(np.concatenate([first8, last8], axis=1), BF16),
        jnp.asarray(spread_rows(), BF16),
        w1,
        b_first[None],
        w_second.reshape(27, 64, 128),
        b_second[None],
        wx,
        jnp.asarray(place_columns(), BF16),
    )

    scale = 1.0 / (T * rows * cols)
    part = lax.all_to_all(terms, "wa", 0, 0, tiled=True)
    part = part.astype(F32).sum(0)
    step = 1
    while step < lax.axis_size("ha"):
        sent = part.astype(BF16)
        pairs = [(i, i ^ step) for i in range(lax.axis_size("ha"))]
        part = sent.astype(F32) + lax.ppermute(sent, "ha", pairs).astype(F32)
        step *= 2
    part = part * scale
    lane = lax.broadcasted_iota(jnp.int32, (128, 16), 0)
    mine = lax.broadcasted_iota(jnp.int32, (128, 16), 1)
    pick = (lane == (mine // 8) * 64 + ha * 8 + mine % 8).astype(F32)
    second = jnp.dot(part[0:120], pick, precision=lax.Precision.HIGHEST, preferred_element_type=F32)
    second = second.reshape(5, 3, 8, 2, 8)
    keep = [TAPS.index((b, c)) for b in range(3) for c in range(3)]
    second = second.transpose(0, 3, 1, 4, 2).reshape(10, 3, 8, 8)
    grad_second = jnp.stack([second[k] for k in keep], axis=1).reshape(3, 3, 3, 8, 8)
    first = part[96:160]
    grad_first = jnp.concatenate([first[0:24, 0:64], first[24:53, 0:64], first[24:53, 64:128]], axis=0)
    grad_first = grad_first[:81].reshape(3, 3, 3, 3, 64)
    return (input_grad, grad_first, grad_second)


def solution(mesh):
    placed = (P(None, None, "ha", "wa"), P(), P(), P(), P(), P(None, "ha", "wa", None))
    return jax.shard_map(
        body,
        mesh=mesh,
        in_specs=placed,
        out_specs=(P(None, None, "ha", "wa"), P(), P(None, None, None, "ha", "wa")),
        check_vma=False,
    )
```

```python
import numpy as np
import jax
import jax.numpy as jnp
from jax import lax
from jax.experimental import pallas as pl
from jax.experimental.pallas import tpu as pltpu
from jax.sharding import PartitionSpec as P

LEAK = 0.2
T = 17
TO = 9
S = 24
F32 = jnp.float32
BF16 = jnp.bfloat16


def dot(a, b):
    return jnp.dot(a, b, preferred_element_type=F32)


def dot_nt(a, b):
    return lax.dot_general(a, b, (((1,), (1,)), ((), ())), preferred_element_type=F32)


HALVES = (0, 1)


def part(k):
    return slice(k * 128, (k + 1) * 128)


def pick_columns():
    m = np.zeros((4, S, 48), np.float32)
    for d in range(4):
        for s in range(22):
            m[d, s, 2 * s + d + 1] = 1
    m = m.reshape(4 * S, 48)
    return m[:, 8:40], m[:, :8], m[:, 40:]


def place_columns():
    m = np.zeros((2, 512, 18, 32), np.float32)
    for p in range(18):
        for s in range(18):
            for co in range(2):
                if 0 <= 2 * s - 3 + co < 32:
                    m[co, p * S + s, p, 2 * s - 3 + co] = 1
    return m.reshape(1024, 576)


def spread_rows():
    m = np.zeros((4, 144, 11, 2, 64), np.float32)
    for d in range(4):
        for q in range(22):
            for k in range(4):
                for ch in range(3):
                    if 2 * q + k + 1 < 48:
                        m[d, ch * 48 + 2 * q + k + 1, q // 2, q % 2, k * 12 + d * 3 + ch] = 1
    return m.reshape(576, 11 * 128)


def first_forward():
    m = np.zeros((3, 128, 2, 4, 81), np.float32)
    for a in range(3):
        for k in range(4):
            for d in range(4):
                for ch in range(3):
                    for rp in range(2):
                        for cp in range(2):
                            b, c = k - rp, d - cp
                            if 0 <= b < 3 and 0 <= c < 3:
                                tap = ((a * 3 + b) * 3 + c) * 3 + ch
                                lane = k * 12 + d * 3 + ch
                                m[a, lane, 0, rp * 2 + cp, tap] = 1
                                m[a, 64 + lane, 1, rp * 2 + cp, tap] = 1
    return m.reshape(384, 2, 4 * 81)


def first_backward():
    m = np.zeros((2, 2, 2, 2, 81, 80), np.float32)
    for di in range(2):
        for dj in range(2):
            for rp in range(2):
                for cp in range(2):
                    for ro in range(2):
                        for co in range(2):
                            b, c = ro + 2 - (2 * di + rp), co + 2 - (2 * dj + cp)
                            if 0 <= b < 3 and 0 <= c < 3:
                                for a in range(3):
                                    for ch in range(3):
                                        tap = ((a * 3 + b) * 3 + c) * 3 + ch
                                        m[di, dj, rp, cp, tap, a * 24 + ro * 12 + co * 3 + ch] = 1
    return m.reshape(16, 81, 80)


BLOCKS = ((1, 1), (1, 2), (2, 1), (2, 2), None, (1, 0), None, (2, 0), (0, 1), (0, 2), None, (0, 0))


def kernel(
    pos, clip, left, right, up, sel_mid, sel_side, spread, w1, b1, w_second, b2, wx, place,
    x_out, g_out,
    ct, p2, mk, sl, hf_a, hf_b, h6_a, h6_b, dacc, sdf, d4, dt, hdf_a, hdf_b, hd4_a, hd4_b, hds, yt, xs, tp, tpt,
    thf_a, thf_b, th6_a, th6_b, oacc, gacc, gf, strips, upf, w2, wb,
):
    r0, c0, rows, cols = pos[0], pos[1], pos[2], pos[3]

    def inside(r, c):
        return (r >= 0) & (r < rows) & (c >= 0) & (c < cols)

    sub = lax.broadcasted_iota(jnp.int32, (S, 256), 0)
    lane = lax.broadcasted_iota(jnp.int32, (S, 256), 1)
    for q in range(22):
        r = r0 + 2 * (q - 3) + (lane >> 7)
        c = c0 + 2 * (sub - 3) + ((lane >> 6) & 1)
        mk[q * S : (q + 1) * S, :] = jnp.where(inside(r, c), 1.0, 0.0)

    p2[0] = jnp.zeros(p2.shape[1:], F32)
    p2[T + 1] = jnp.zeros(p2.shape[1:], F32)
    yt[T + 2] = jnp.zeros(yt.shape[1:], F32)
    tp[...] = jnp.zeros(tp.shape, BF16)
    tpt[0] = jnp.zeros(tpt.shape[1:], BF16)
    tpt[T + 1] = jnp.zeros(tpt.shape[1:], BF16)
    oacc[...] = jnp.zeros(oacc.shape, F32)
    gacc[...] = jnp.zeros(gacc.shape, F32)
    sdf[480:496, :] = jnp.zeros((16, 128), F32)
    gf[...] = jnp.zeros(gf.shape, F32)
    upf[...] = jnp.zeros(upf.shape, F32)

    for n, a in enumerate((2, 0, 1)):
        for k, tap in enumerate(BLOCKS):
            block = jnp.zeros((64, 128), BF16) if tap is None else w_second[a * 9 + tap[0] * 3 + tap[1]]
            w2[k * 64 : (k + 1) * 64, n * 128 : (n + 1) * 128] = block
    for n, a in enumerate((1, 2, 0)):
        for dq in range(2):
            for ds in range(2):
                for rp in range(2):
                    b = rp + 1 - 2 * dq
                    pair = jnp.zeros((128, 128), F32)
                    if b >= 0:
                        taps = [w_second[a * 9 + b * 3 + c].astype(F32) for c in ((0,) if ds else (1, 2))]
                        pair = jnp.concatenate([jnp.zeros((64, 128), F32)] * ds + taps, axis=0)
                    to = (n * 4 + dq * 2 + ds) * 128
                    wb[to : to + 128, rp * 128 : (rp + 1) * 128] = jnp.transpose(pair).astype(BF16)

    strips[0] = jnp.where(c0 > 0, left[...].astype(F32), 0.0)
    strips[1] = jnp.where(c0 + 32 < cols, right[...].astype(F32), 0.0)
    h6_b[...] = jnp.zeros(h6_b.shape, BF16)
    hd4_b[...] = jnp.zeros(hd4_b.shape, BF16)
    hds[0] = jnp.zeros(hds.shape[1:], BF16)
    th6_b[...] = jnp.zeros(th6_b.shape, BF16)

    @pl.loop(0, T, unroll=True)
    def _(t):
        middle = jnp.concatenate([clip[0, t], clip[1, t], clip[2, t]], axis=0)
        edges = jnp.concatenate(
            [
                jnp.concatenate(
                    [strips[k, pl.ds(pl.multiple_of((ch * T + t) * 8, 8), 8), 0:48] for ch in range(3)], axis=1
                )
                for k in range(2)
            ],
            axis=0,
        ).astype(BF16)
        turned = dot_nt(sel_mid[...], middle) + dot(sel_side[...], edges)
        at = pl.ds(pl.multiple_of(t * S, 8), S)
        for d in range(4):
            ct[at, d * 144 : (d + 1) * 144] = turned[d * S : (d + 1) * S]

    for n in range(0, 11, 2):
        width = min(2, 11 - n) * 128
        window = dot(ct[...].astype(BF16), spread[:, n * 128 : n * 128 + width])
        for k in range(width // 128):
            q = n + k
            p2[1 : T + 1, q * S : (q + 1) * S, :] = window[:, part(k)].reshape(T, S, 128)

    for p in range(TO + 1):
        dacc[p] = jnp.broadcast_to(b2[...], (480, 128))

    def hidden(t, hf, h6):
        lhs = jnp.concatenate([p2[t], p2[t + 1], p2[t + 2]], axis=1).astype(BF16)
        pre = dot(lhs, w1[...]) + jnp.concatenate([b1[...]] * 8, axis=1)
        slope = jnp.where(pre > 0, 1.0, LEAK)
        for q in range(11):
            for e in range(2):
                to = slice((2 * q + e) * S, (2 * q + e + 1) * S)
                of = (slice(q * S, (q + 1) * S), slice(e * 256, (e + 1) * 256))
                masked = slope[of] * mk[to, :]
                active = pre[of] * masked
                for h in HALVES:
                    sl[t, h, to, :] = masked[:, part(h)]
                    hf[h, to, :] = active[:, part(h)]
        for h in HALVES:
            h6[:, part(h)] = hf[h, 25:505, :].astype(BF16)
            h6[:, part(h + 2)] = hf[h, 24:504, :].astype(BF16)
        h6[:, 512:640] = hf[1, 1:481, :].astype(BF16)
        h6[:, 640:768] = hf[1, 0:480, :].astype(BF16)

    def odd_second(p):
        both = dot(h6_b[...], w2[:, 0:256])
        dacc[p + 1] += both[:, 0:128]
        dacc[p + 2] += both[:, 128:256]

    def even_second(p):
        dacc[p + 1] += dot(h6_a[...], w2[:, 256:384])

    @pl.loop(0, TO - 1, unroll=True)
    def _(p):
        hidden(2 * p, hf_a, h6_a)
        odd_second(p - 1)
        hidden(2 * p + 1, hf_b, h6_b)
        even_second(p)

    hidden(2 * TO - 2, hf_a, h6_a)
    odd_second(TO - 2)
    even_second(TO - 1)

    at384 = lax.broadcasted_iota(jnp.int32, (384, 128), 0)
    core = jnp.where(at384 % S < 16, 1.0, 0.0)

    for p in range(TO):
        slope = jnp.where(dacc[p + 1] > 0, 1.0, LEAK)
        for q in range(20):
            upf[q * S + 2 : q * S + 18, :] = up[p, q].astype(F32)
        for s in range(2):
            of = slice(408 + (p * 2 + s) * 20, 428 + (p * 2 + s) * 20)
            upf[pl.ds(s, 20, stride=S), :] = strips[0, of, :]
            upf[pl.ds(18 + s, 20, stride=S), :] = strips[1, of, :]
        sdf[0:480, :] = upf[...] * slope
        d4[p, :, 0:128] = sdf[0:464, :].astype(BF16)
        d4[p, :, 128:256] = sdf[1:465, :].astype(BF16)
        d4[p, :, 256:384] = sdf[24:488, :].astype(BF16)
        d4[p, :, 384:512] = sdf[25:489, :].astype(BF16)
        dt[p] = jnp.transpose(sdf[50:434, :] * core).astype(BF16)

    def delta(t, back, hdf, hd4):
        for h in HALVES:
            hdf[h] = back[:, part(h)] * sl[t, h, 25:489, :]
        for h in HALVES:
            hds[t + 1, :, part(h)] = hdf[h, 25:457, :].astype(BF16)
            hd4[:, part(h)] = hdf[h, 0:432, :].astype(BF16)
            hd4[:, part(h + 2)] = hdf[h, 1:433, :].astype(BF16)
            hd4[:, part(h + 4)] = hdf[h, 24:456, :].astype(BF16)

    def products(t, hd4):
        yt[t + 2, :, 0:432] = dot_nt(wx[:, 0:768], hd4[...]) + dot_nt(wx[:, 768:1024], hds[t + 1])

    @pl.loop(0, TO - 1, unroll=True)
    def _(p):
        delta(2 * p, dot(d4[p], wb[0:512, :]), hdf_a, hd4_a)
        products(2 * p - 1, hd4_b)
        lhs = jnp.concatenate([d4[p], d4[p + 1]], axis=1)
        delta(2 * p + 1, dot(lhs, wb[512:1536, :]), hdf_b, hd4_b)
        products(2 * p, hd4_a)

    delta(2 * TO - 2, dot(d4[TO - 1], wb[0:512, :]), hdf_a, hd4_a)
    products(2 * TO - 3, hd4_b)
    products(2 * TO - 2, hd4_a)

    index = lax.broadcasted_iota(jnp.int32, (S, 512), 0)
    cell = lax.broadcasted_iota(jnp.int32, (S, 512), 1)
    second_row = index >= 12
    in_row = jnp.where(second_row, index - 12, index)
    r = r0 + 2 * (cell // S) - 3 + jnp.where(second_row, 1, 0)
    c = c0 + 2 * (cell % S) - 3 + jnp.where(in_row >= 3, 1, 0)
    live = inside(r, c) & (in_row < 6) & (cell < 432)
    cell = lax.broadcasted_iota(jnp.int32, (48, 416), 1)
    core_first = (cell % S >= 1) & (cell % S <= 16) & (cell >= S) & (cell < 17 * S)
    cell = lax.broadcasted_iota(jnp.int32, (S, 512), 1)

    @pl.loop(0, T, unroll=True)
    def _(t):
        x = yt[t + 3, 0:24, :] + yt[t + 2, 24:48, :] + yt[t + 1, 48:72, :]
        x = jnp.where(cell < 432, x, 0.0)
        at = pl.ds(pl.multiple_of(t * 48, 16), 48)
        for co in range(2):
            here = x if co == 0 else pltpu.roll(x, 21, 0)
            high = here.astype(BF16).astype(F32)
            xs[at, co * 512 : (co + 1) * 512] = jnp.concatenate([high, here - high], axis=0).astype(BF16)
        m = jnp.where(live, x, 0.0)
        upper = m + pltpu.roll(pltpu.roll(m, 511, 1), 6, 0)
        lower = pltpu.roll(m, 488, 1) + pltpu.roll(pltpu.roll(m, 487, 1), 6, 0)
        wide = jnp.concatenate([upper, lower], axis=0)
        tpt[t + 1] = jnp.where(core_first, wide[:, 0:416], 0.0).astype(BF16)
        tp[t + 1, :, 0:48] = jnp.transpose(wide)[0:416].astype(BF16)

    for first in range(0, T, 6):
        frames = range(first, min(first + 6, T))
        group = dot(xs[first * 48 : (frames[-1] + 1) * 48, :], place[...])
        for n in frames:
            at = (n - first) * 48
            placed = group[at : at + 24] + group[at + 24 : at + 48]
            for p in range(18):
                for ro in range(2):
                    row = 2 * p - 3 + ro
                    if 0 <= row < 32:
                        for ch in range(3):
                            k = ro * 12 + ch
                            x_out[ch, n, row : row + 1, :] = placed[k : k + 1, p * 32 : p * 32 + 32]

    def tangents(t, thf, th6):
        lhs = jnp.concatenate([tp[t], tp[t + 1], tp[t + 2]], axis=1)
        raw = dot(lhs, w1[:, 0:256])
        for h in HALVES:
            thf[h] = raw[:, part(h)] * sl[t, h, 50:466, :]
        for h in HALVES:
            th6[:, part(h)] = thf[h, 25:409, :].astype(BF16)
            th6[:, part(h + 2)] = thf[h, 24:408, :].astype(BF16)
        th6[:, 512:640] = thf[1, 1:385, :].astype(BF16)
        th6[:, 640:768] = thf[1, 0:384, :].astype(BF16)
        turned = jnp.concatenate([tpt[t], tpt[t + 1], tpt[t + 2]], axis=0)
        gacc[...] += dot(turned, hds[t + 1, 0:416, :])

    def odd_terms(p):
        both = dot(dt[pl.ds(jnp.maximum(p, 0), 2)].reshape(256, 384), th6_b[...])
        oacc[256:384, :] += both[0:128]
        oacc[0:128, :] += both[128:256]

    def even_terms(p):
        oacc[128:256, :] += dot(dt[p], th6_a[...])

    @pl.loop(0, TO - 1, unroll=True)
    def _(p):
        tangents(2 * p, thf_a, th6_a)
        odd_terms(p - 1)
        tangents(2 * p + 1, thf_b, th6_b)
        even_terms(p)

    tangents(2 * TO - 2, thf_a, th6_a)
    odd_terms(TO - 2)
    even_terms(TO - 1)

    for a in range(3):
        for b in range(3):
            total = jnp.zeros((9, 64), F32)
            for rp in range(2):
                for cp in range(2):
                    start = a * 48 + (b + rp) * 12 + cp * 3
                    tap = (rp * 2 + cp) * 64
                    total += gacc[start : start + 9, tap : tap + 64]
            gf[a * 27 + b * 9 : a * 27 + b * 9 + 9, :] = total

    left_half = lax.broadcasted_iota(jnp.int32, (8, 128), 1) < 64
    ends = jnp.concatenate([gf[24:56, :], gf[53:85, :]], axis=1)
    ends = jnp.concatenate([ends, jnp.zeros((8, 128), F32)], axis=0)
    start = jnp.concatenate([gf[0:24, :], jnp.zeros((24, 64), F32)], axis=1)
    for w in range(16):
        tiles = [[oacc[a * 128 + w * 8 : a * 128 + w * 8 + 8, k * 128 : k * 128 + 128] for a in range(3)] for k in range(6)]
        mixed = [jnp.where(left_half, pltpu.roll(tiles[2][a], 64, 1), tiles[3][a]) for a in range(3)]
        last = [jnp.where(left_half, start[a * 8 : a * 8 + 8], tiles[5][a]) for a in range(3)]
        g_out[w] = jnp.concatenate(tiles[0] + tiles[1] + mixed + tiles[4] + last + [ends], axis=0).astype(BF16)


TAPS = ((1, 1), (1, 2), (2, 1), (2, 2), (1, 0), (2, 0), (0, 1), (0, 2), None, (0, 0))


def run_kernel(*args):
    vm = lambda shape, kind=F32: pltpu.VMEM(shape, kind)
    vmem = pl.BlockSpec(memory_space=pltpu.VMEM)
    return pl.pallas_call(
        kernel,
        out_shape=(
            jax.ShapeDtypeStruct((3, T, 32, 32), F32),
            jax.ShapeDtypeStruct((16, 160, 128), BF16),
        ),
        in_specs=[pl.BlockSpec(memory_space=pltpu.SMEM)] + [vmem] * 13,
        out_specs=(vmem, vmem),
        scratch_shapes=[
            vm((T * S, 576)),
            vm((T + 2, 264, 128)),
            vm((528, 256)),
            vm((T, 2, 528, 128)),
            vm((2, 528, 128)),
            vm((2, 528, 128)),
            vm((480, 768), BF16),
            vm((480, 768), BF16),
            vm((TO + 1, 480, 128)),
            vm((496, 128)),
            vm((TO, 464, 512), BF16),
            vm((TO, 128, 384), BF16),
            vm((2, 464, 128)),
            vm((2, 464, 128)),
            vm((432, 768), BF16),
            vm((432, 768), BF16),
            vm((T + 1, 432, 256), BF16),
            vm((T + 3, 80, 512)),
            vm((T * 48, 1024), BF16),
            vm((T + 2, 416, 128), BF16),
            vm((T + 2, 48, 416), BF16),
            vm((2, 416, 128)),
            vm((2, 416, 128)),
            vm((384, 768), BF16),
            vm((384, 768), BF16),
            vm((384, 768)),
            vm((144, 256)),
            vm((96, 64)),
            vm((2, 768, 128)),
            vm((480, 128)),
            vm((768, 384), BF16),
            vm((1536, 256), BF16),
        ],
        compiler_params=pltpu.CompilerParams(vmem_limit_bytes=60 * 1024 * 1024),
        cost_estimate=pl.CostEstimate(flops=10**10, bytes_accessed=2 * 10**7, transcendentals=0),
    )(*args)


def swapped(to_next, to_prev, axis):
    size = lax.axis_size(axis)
    ring = [(i, (i + 1) % size) for i in range(size)]
    return lax.ppermute(to_next, axis, ring), lax.ppermute(to_prev, axis, [(j, i) for i, j in ring])


def packed(clip_part, up_part):
    flat = clip_part.reshape(408, clip_part.shape[3])
    flat = jnp.pad(flat, ((0, 0), (0, 128 - flat.shape[1])))
    return jnp.concatenate([flat, up_part.reshape(-1, 128)], axis=0)


def body(clip, w_first, b_first, w_second, b_second, upstream):
    rows = clip.shape[2] * lax.axis_size("ha")
    cols = clip.shape[3] * lax.axis_size("wa")
    ha, wa = lax.axis_index("ha"), lax.axis_index("wa")
    pos = jnp.stack([ha * 32, wa * 32, jnp.int32(rows), jnp.int32(cols)]).astype(jnp.int32)

    above, below = swapped(
        packed(clip[:, :, 24:32], upstream[:, 14:16]), packed(clip[:, :, 0:8], upstream[:, 0:2]), "ha"
    )
    above = jnp.where(ha > 0, above, jnp.zeros_like(above))
    below = jnp.where(ha < lax.axis_size("ha") - 1, below, jnp.zeros_like(below))
    clip_part = lambda v, width: v[:408, :width].reshape(3, T, 8, width)
    clip_rows = jnp.concatenate([clip_part(above, 32), clip, clip_part(below, 32)], axis=2)
    up_part = lambda v: v[408:].reshape(TO, 2, 16, 128)
    up_rows = jnp.concatenate([up_part(above), upstream, up_part(below)], axis=1)
    left, right = swapped(
        packed(jnp.swapaxes(clip_rows[:, :, :, 24:32], 2, 3), jnp.swapaxes(up_rows[:, :, 14:16], 1, 2)),
        packed(jnp.swapaxes(clip_rows[:, :, :, 0:8], 2, 3), jnp.swapaxes(up_rows[:, :, 0:2], 1, 2)),
        "wa",
    )

    w_flat = w_first.reshape(81, 64)
    diagonal = jnp.concatenate(
        [jnp.pad(w_flat, ((0, 0), (64 * k, 192 - 64 * k))) for k in range(4)], axis=0
    )
    forward_pick = jnp.asarray(first_forward(), BF16)
    w1 = jnp.concatenate(
        [dot(forward_pick[:, e], diagonal).astype(BF16) for e in range(2)], axis=1
    )
    wx = jnp.einsum(
        "ko,bkl->lbo", w_flat, jnp.asarray(first_backward(), BF16), preferred_element_type=F32
    )
    wx = wx.astype(BF16).reshape(80, 1024)
    middle, first8, last8 = pick_columns()
    input_grad, terms = run_kernel(
        pos,
        clip_rows,
        left,
        right,
        up_rows,
        jnp.asarray(middle, BF16),
        jnp.asarray(np.concatenate([first8, last8], axis=1), BF16),
        jnp.asarray(spread_rows(), BF16),
        w1,
        b_first[None],
        w_second.reshape(27, 64, 128),
        b_second[None],
        wx,
        jnp.asarray(place_columns(), BF16),
    )

    scale = 1.0 / (T * rows * cols)
    terms = lax.all_to_all(terms, "wa", 0, 0, tiled=True)
    terms = terms.astype(F32).sum(0)
    step = 1
    while step < lax.axis_size("ha"):
        sent = terms.astype(BF16)
        pairs = [(i, i ^ step) for i in range(lax.axis_size("ha"))]
        terms = sent.astype(F32) + lax.ppermute(sent, "ha", pairs).astype(F32)
        step *= 2
    terms = terms * scale
    lane = lax.broadcasted_iota(jnp.int32, (128, 16), 0)
    mine = lax.broadcasted_iota(jnp.int32, (128, 16), 1)
    pick = (lane == (mine // 8) * 64 + ha * 8 + mine % 8).astype(F32)
    second = jnp.dot(terms[0:120], pick, precision=lax.Precision.HIGHEST, preferred_element_type=F32)
    second = second.reshape(5, 3, 8, 2, 8)
    keep = [TAPS.index((b, c)) for b in range(3) for c in range(3)]
    second = second.transpose(0, 3, 1, 4, 2).reshape(10, 3, 8, 8)
    grad_second = jnp.stack([second[k] for k in keep], axis=1).reshape(3, 3, 3, 8, 8)
    first = terms[96:160]
    grad_first = jnp.concatenate([first[0:24, 0:64], first[24:53, 0:64], first[24:53, 64:128]], axis=0)
    grad_first = grad_first[:81].reshape(3, 3, 3, 3, 64)
    return (input_grad, grad_first, grad_second)


def solution(mesh):
    placed = (P(None, None, "ha", "wa"), P(), P(), P(), P(), P(None, "ha", "wa", None))
    return jax.shard_map(
        body,
        mesh=mesh,
        in_specs=placed,
        out_specs=(P(None, None, "ha", "wa"), P(), P(None, None, None, "ha", "wa")),
        check_vma=False,
    )
```

```python
import numpy as np
import jax
import jax.numpy as jnp
from jax import lax
from jax.experimental import pallas as pl
from jax.experimental.pallas import tpu as pltpu
from jax.sharding import PartitionSpec as P

LEAK = 0.2
T = 17
TO = 9
S = 24
F32 = jnp.float32
BF16 = jnp.bfloat16


def dot(a, b):
    return jnp.dot(a, b, preferred_element_type=F32)


def dot_nt(a, b):
    return lax.dot_general(a, b, (((1,), (1,)), ((), ())), preferred_element_type=F32)


HALVES = (0, 1)


def part(k):
    return slice(k * 128, (k + 1) * 128)


def pick_columns():
    m = np.zeros((4, S, 48), np.float32)
    for d in range(4):
        for s in range(22):
            m[d, s, 2 * s + d + 1] = 1
    m = m.reshape(4 * S, 48)
    return m[:, 8:40], m[:, :8], m[:, 40:]


def place_columns():
    m = np.zeros((2, 512, 18, 32), np.float32)
    for p in range(18):
        for s in range(18):
            for co in range(2):
                if 0 <= 2 * s - 3 + co < 32:
                    m[co, p * S + s, p, 2 * s - 3 + co] = 1
    return m.reshape(1024, 576)


def spread_rows():
    m = np.zeros((4, 144, 11, 2, 64), np.float32)
    for d in range(4):
        for q in range(22):
            for k in range(4):
                for ch in range(3):
                    if 2 * q + k + 1 < 48:
                        m[d, ch * 48 + 2 * q + k + 1, q // 2, q % 2, k * 12 + d * 3 + ch] = 1
    return m.reshape(576, 11 * 128)


def first_forward():
    m = np.zeros((3, 128, 2, 4, 81), np.float32)
    for a in range(3):
        for k in range(4):
            for d in range(4):
                for ch in range(3):
                    for rp in range(2):
                        for cp in range(2):
                            b, c = k - rp, d - cp
                            if 0 <= b < 3 and 0 <= c < 3:
                                tap = ((a * 3 + b) * 3 + c) * 3 + ch
                                lane = k * 12 + d * 3 + ch
                                m[a, lane, 0, rp * 2 + cp, tap] = 1
                                m[a, 64 + lane, 1, rp * 2 + cp, tap] = 1
    return m.reshape(384, 2, 4 * 81)


def first_backward():
    m = np.zeros((2, 2, 2, 2, 81, 80), np.float32)
    for di in range(2):
        for dj in range(2):
            for rp in range(2):
                for cp in range(2):
                    for ro in range(2):
                        for co in range(2):
                            b, c = ro + 2 - (2 * di + rp), co + 2 - (2 * dj + cp)
                            if 0 <= b < 3 and 0 <= c < 3:
                                for a in range(3):
                                    for ch in range(3):
                                        tap = ((a * 3 + b) * 3 + c) * 3 + ch
                                        m[di, dj, rp, cp, tap, a * 24 + ro * 12 + co * 3 + ch] = 1
    return m.reshape(16, 81, 80)


BLOCKS = ((1, 1), (1, 2), (2, 1), (2, 2), None, (1, 0), None, (2, 0), (0, 1), (0, 2), None, (0, 0))


def kernel(
    pos, clip, left, right, up_far, sel_mid, sel_side, spread, w1, b1, w_second, b2, wx, place_far,
    x_out, g_out,
    ct, p2, mk, sl, hf_a, hf_b, h6_a, h6_b, dacc, sdf, d4, dt, hdf_a, hdf_b, hd4_a, hd4_b, hds, yt, xs, tp, tpt,
    thf_a, thf_b, th6_a, th6_b, oacc, gacc, gf, strips, upf, w2, wb, near, up, place, sems,
):
    copies = [
        pltpu.make_async_copy(left, near.at[0], sems.at[0]),
        pltpu.make_async_copy(right, near.at[1], sems.at[1]),
        pltpu.make_async_copy(up_far, up, sems.at[2]),
        pltpu.make_async_copy(place_far, place, sems.at[3]),
    ]
    for copy in copies:
        copy.start()
    r0, c0, rows, cols = pos[0], pos[1], pos[2], pos[3]

    def inside(r, c):
        return (r >= 0) & (r < rows) & (c >= 0) & (c < cols)

    sub = lax.broadcasted_iota(jnp.int32, (S, 256), 0)
    lane = lax.broadcasted_iota(jnp.int32, (S, 256), 1)
    for q in range(22):
        r = r0 + 2 * (q - 3) + (lane >> 7)
        c = c0 + 2 * (sub - 3) + ((lane >> 6) & 1)
        mk[q * S : (q + 1) * S, :] = jnp.where(inside(r, c), 1.0, 0.0)

    p2[0] = jnp.zeros(p2.shape[1:], F32)
    p2[T + 1] = jnp.zeros(p2.shape[1:], F32)
    yt[T + 2] = jnp.zeros(yt.shape[1:], F32)
    tp[...] = jnp.zeros(tp.shape, BF16)
    tpt[0] = jnp.zeros(tpt.shape[1:], BF16)
    tpt[T + 1] = jnp.zeros(tpt.shape[1:], BF16)
    oacc[...] = jnp.zeros(oacc.shape, F32)
    gacc[...] = jnp.zeros(gacc.shape, F32)
    sdf[480:496, :] = jnp.zeros((16, 128), F32)
    gf[...] = jnp.zeros(gf.shape, F32)
    upf[...] = jnp.zeros(upf.shape, F32)

    for n, a in enumerate((2, 0, 1)):
        for k, tap in enumerate(BLOCKS):
            block = jnp.zeros((64, 128), BF16) if tap is None else w_second[a * 9 + tap[0] * 3 + tap[1]]
            w2[k * 64 : (k + 1) * 64, n * 128 : (n + 1) * 128] = block
    for n, a in enumerate((1, 2, 0)):
        for dq in range(2):
            for ds in range(2):
                for rp in range(2):
                    b = rp + 1 - 2 * dq
                    pair = jnp.zeros((128, 128), F32)
                    if b >= 0:
                        taps = [w_second[a * 9 + b * 3 + c].astype(F32) for c in ((0,) if ds else (1, 2))]
                        pair = jnp.concatenate([jnp.zeros((64, 128), F32)] * ds + taps, axis=0)
                    to = (n * 4 + dq * 2 + ds) * 128
                    wb[to : to + 128, rp * 128 : (rp + 1) * 128] = jnp.transpose(pair).astype(BF16)

    h6_b[...] = jnp.zeros(h6_b.shape, BF16)
    hd4_b[...] = jnp.zeros(hd4_b.shape, BF16)
    hds[0] = jnp.zeros(hds.shape[1:], BF16)
    th6_b[...] = jnp.zeros(th6_b.shape, BF16)

    copies[0].wait()
    copies[1].wait()
    strips[0] = jnp.where(c0 > 0, near[0].astype(F32), 0.0)
    strips[1] = jnp.where(c0 + 32 < cols, near[1].astype(F32), 0.0)

    @pl.loop(0, T, unroll=True)
    def _(t):
        middle = jnp.concatenate([clip[0, t], clip[1, t], clip[2, t]], axis=0)
        edges = jnp.concatenate(
            [
                jnp.concatenate(
                    [strips[k, pl.ds(pl.multiple_of((ch * T + t) * 8, 8), 8), 0:48] for ch in range(3)], axis=1
                )
                for k in range(2)
            ],
            axis=0,
        ).astype(BF16)
        turned = dot_nt(sel_mid[...], middle) + dot(sel_side[...], edges)
        at = pl.ds(pl.multiple_of(t * S, 8), S)
        for d in range(4):
            ct[at, d * 144 : (d + 1) * 144] = turned[d * S : (d + 1) * S]

    for n in range(0, 11, 2):
        width = min(2, 11 - n) * 128
        window = dot(ct[...].astype(BF16), spread[:, n * 128 : n * 128 + width])
        for k in range(width // 128):
            q = n + k
            p2[1 : T + 1, q * S : (q + 1) * S, :] = window[:, part(k)].reshape(T, S, 128)

    for p in range(TO + 1):
        dacc[p] = jnp.broadcast_to(b2[...], (480, 128))

    def hidden(t, hf, h6):
        lhs = jnp.concatenate([p2[t], p2[t + 1], p2[t + 2]], axis=1).astype(BF16)
        pre = dot(lhs, w1[...]) + jnp.concatenate([b1[...]] * 8, axis=1)
        slope = jnp.where(pre > 0, 1.0, LEAK)
        for q in range(11):
            for e in range(2):
                to = slice((2 * q + e) * S, (2 * q + e + 1) * S)
                of = (slice(q * S, (q + 1) * S), slice(e * 256, (e + 1) * 256))
                masked = slope[of] * mk[to, :]
                active = pre[of] * masked
                for h in HALVES:
                    sl[t, h, to, :] = masked[:, part(h)]
                    hf[h, to, :] = active[:, part(h)]
        for h in HALVES:
            h6[:, part(h)] = hf[h, 25:505, :].astype(BF16)
            h6[:, part(h + 2)] = hf[h, 24:504, :].astype(BF16)
        h6[:, 512:640] = hf[1, 1:481, :].astype(BF16)
        h6[:, 640:768] = hf[1, 0:480, :].astype(BF16)

    def odd_second(p):
        both = dot(h6_b[...], w2[:, 0:256])
        dacc[p + 1] += both[:, 0:128]
        dacc[p + 2] += both[:, 128:256]

    def even_second(p):
        dacc[p + 1] += dot(h6_a[...], w2[:, 256:384])

    @pl.loop(0, TO - 1, unroll=True)
    def _(p):
        hidden(2 * p, hf_a, h6_a)
        odd_second(p - 1)
        hidden(2 * p + 1, hf_b, h6_b)
        even_second(p)

    hidden(2 * TO - 2, hf_a, h6_a)
    odd_second(TO - 2)
    even_second(TO - 1)

    at384 = lax.broadcasted_iota(jnp.int32, (384, 128), 0)
    core = jnp.where(at384 % S < 16, 1.0, 0.0)

    copies[2].wait()
    for p in range(TO):
        slope = jnp.where(dacc[p + 1] > 0, 1.0, LEAK)
        for q in range(20):
            upf[q * S + 2 : q * S + 18, :] = up[p, q].astype(F32)
        for s in range(2):
            of = slice(408 + (p * 2 + s) * 20, 428 + (p * 2 + s) * 20)
            upf[pl.ds(s, 20, stride=S), :] = strips[0, of, :]
            upf[pl.ds(18 + s, 20, stride=S), :] = strips[1, of, :]
        sdf[0:480, :] = upf[...] * slope
        d4[p, :, 0:128] = sdf[0:464, :].astype(BF16)
        d4[p, :, 128:256] = sdf[1:465, :].astype(BF16)
        d4[p, :, 256:384] = sdf[24:488, :].astype(BF16)
        d4[p, :, 384:512] = sdf[25:489, :].astype(BF16)
        dt[p] = jnp.transpose(sdf[50:434, :] * core).astype(BF16)

    def delta(t, back, hdf, hd4):
        for h in HALVES:
            hdf[h] = back[:, part(h)] * sl[t, h, 25:489, :]
        for h in HALVES:
            hds[t + 1, :, part(h)] = hdf[h, 25:457, :].astype(BF16)
            hd4[:, part(h)] = hdf[h, 0:432, :].astype(BF16)
            hd4[:, part(h + 2)] = hdf[h, 1:433, :].astype(BF16)
            hd4[:, part(h + 4)] = hdf[h, 24:456, :].astype(BF16)

    def products(t, hd4):
        yt[t + 2, :, 0:432] = dot_nt(wx[:, 0:768], hd4[...]) + dot_nt(wx[:, 768:1024], hds[t + 1])

    @pl.loop(0, TO - 1, unroll=True)
    def _(p):
        delta(2 * p, dot(d4[p], wb[0:512, :]), hdf_a, hd4_a)
        products(2 * p - 1, hd4_b)
        lhs = jnp.concatenate([d4[p], d4[p + 1]], axis=1)
        delta(2 * p + 1, dot(lhs, wb[512:1536, :]), hdf_b, hd4_b)
        products(2 * p, hd4_a)

    delta(2 * TO - 2, dot(d4[TO - 1], wb[0:512, :]), hdf_a, hd4_a)
    products(2 * TO - 3, hd4_b)
    products(2 * TO - 2, hd4_a)

    index = lax.broadcasted_iota(jnp.int32, (S, 512), 0)
    cell = lax.broadcasted_iota(jnp.int32, (S, 512), 1)
    second_row = index >= 12
    in_row = jnp.where(second_row, index - 12, index)
    r = r0 + 2 * (cell // S) - 3 + jnp.where(second_row, 1, 0)
    c = c0 + 2 * (cell % S) - 3 + jnp.where(in_row >= 3, 1, 0)
    live = inside(r, c) & (in_row < 6) & (cell < 432)
    cell = lax.broadcasted_iota(jnp.int32, (48, 416), 1)
    core_first = (cell % S >= 1) & (cell % S <= 16) & (cell >= S) & (cell < 17 * S)
    cell = lax.broadcasted_iota(jnp.int32, (S, 512), 1)

    @pl.loop(0, T, unroll=True)
    def _(t):
        x = yt[t + 3, 0:24, :] + yt[t + 2, 24:48, :] + yt[t + 1, 48:72, :]
        x = jnp.where(cell < 432, x, 0.0)
        at = pl.ds(pl.multiple_of(t * 48, 16), 48)
        for co in range(2):
            here = x if co == 0 else pltpu.roll(x, 21, 0)
            high = here.astype(BF16).astype(F32)
            xs[at, co * 512 : (co + 1) * 512] = jnp.concatenate([high, here - high], axis=0).astype(BF16)
        m = jnp.where(live, x, 0.0)
        upper = m + pltpu.roll(pltpu.roll(m, 511, 1), 6, 0)
        lower = pltpu.roll(m, 488, 1) + pltpu.roll(pltpu.roll(m, 487, 1), 6, 0)
        wide = jnp.concatenate([upper, lower], axis=0)
        tpt[t + 1] = jnp.where(core_first, wide[:, 0:416], 0.0).astype(BF16)
        tp[t + 1, :, 0:48] = jnp.transpose(wide)[0:416].astype(BF16)

    copies[3].wait()
    for first in range(0, T, 6):
        frames = range(first, min(first + 6, T))
        group = dot(xs[first * 48 : (frames[-1] + 1) * 48, :], place[...])
        for n in frames:
            at = (n - first) * 48
            placed = group[at : at + 24] + group[at + 24 : at + 48]
            for p in range(18):
                for ro in range(2):
                    row = 2 * p - 3 + ro
                    if 0 <= row < 32:
                        for ch in range(3):
                            k = ro * 12 + ch
                            x_out[ch, n, row : row + 1, :] = placed[k : k + 1, p * 32 : p * 32 + 32]

    def tangents(t, thf, th6):
        lhs = jnp.concatenate([tp[t], tp[t + 1], tp[t + 2]], axis=1)
        raw = dot(lhs, w1[:, 0:256])
        for h in HALVES:
            thf[h] = raw[:, part(h)] * sl[t, h, 50:466, :]
        for h in HALVES:
            th6[:, part(h)] = thf[h, 25:409, :].astype(BF16)
            th6[:, part(h + 2)] = thf[h, 24:408, :].astype(BF16)
        th6[:, 512:640] = thf[1, 1:385, :].astype(BF16)
        th6[:, 640:768] = thf[1, 0:384, :].astype(BF16)
        turned = jnp.concatenate([tpt[t], tpt[t + 1], tpt[t + 2]], axis=0)
        gacc[...] += dot(turned, hds[t + 1, 0:416, :])

    def odd_terms(p):
        both = dot(dt[pl.ds(jnp.maximum(p, 0), 2)].reshape(256, 384), th6_b[...])
        oacc[256:384, :] += both[0:128]
        oacc[0:128, :] += both[128:256]

    def even_terms(p):
        oacc[128:256, :] += dot(dt[p], th6_a[...])

    @pl.loop(0, TO - 1, unroll=True)
    def _(p):
        tangents(2 * p, thf_a, th6_a)
        odd_terms(p - 1)
        tangents(2 * p + 1, thf_b, th6_b)
        even_terms(p)

    tangents(2 * TO - 2, thf_a, th6_a)
    odd_terms(TO - 2)
    even_terms(TO - 1)

    for a in range(3):
        for b in range(3):
            total = jnp.zeros((9, 64), F32)
            for rp in range(2):
                for cp in range(2):
                    start = a * 48 + (b + rp) * 12 + cp * 3
                    tap = (rp * 2 + cp) * 64
                    total += gacc[start : start + 9, tap : tap + 64]
            gf[a * 27 + b * 9 : a * 27 + b * 9 + 9, :] = total

    left_half = lax.broadcasted_iota(jnp.int32, (8, 128), 1) < 64
    ends = jnp.concatenate([gf[24:56, :], gf[53:85, :]], axis=1)
    ends = jnp.concatenate([ends, jnp.zeros((8, 128), F32)], axis=0)
    start = jnp.concatenate([gf[0:24, :], jnp.zeros((24, 64), F32)], axis=1)
    for w in range(16):
        tiles = [[oacc[a * 128 + w * 8 : a * 128 + w * 8 + 8, k * 128 : k * 128 + 128] for a in range(3)] for k in range(6)]
        mixed = [jnp.where(left_half, pltpu.roll(tiles[2][a], 64, 1), tiles[3][a]) for a in range(3)]
        last = [jnp.where(left_half, start[a * 8 : a * 8 + 8], tiles[5][a]) for a in range(3)]
        g_out[w] = jnp.concatenate(tiles[0] + tiles[1] + mixed + tiles[4] + last + [ends], axis=0).astype(BF16)


TAPS = ((1, 1), (1, 2), (2, 1), (2, 2), (1, 0), (2, 0), (0, 1), (0, 2), None, (0, 0))


def run_kernel(*args):
    vm = lambda shape, kind=F32: pltpu.VMEM(shape, kind)
    vmem = pl.BlockSpec(memory_space=pltpu.VMEM)
    far = pl.BlockSpec(memory_space=pl.ANY)
    return pl.pallas_call(
        kernel,
        out_shape=(
            jax.ShapeDtypeStruct((3, T, 32, 32), F32),
            jax.ShapeDtypeStruct((16, 160, 128), BF16),
        ),
        in_specs=[pl.BlockSpec(memory_space=pltpu.SMEM)] + [vmem, far, far, far] + [vmem] * 8 + [far],
        out_specs=(vmem, vmem),
        scratch_shapes=[
            vm((T * S, 576)),
            vm((T + 2, 264, 128)),
            vm((528, 256)),
            vm((T, 2, 528, 128)),
            vm((2, 528, 128)),
            vm((2, 528, 128)),
            vm((480, 768), BF16),
            vm((480, 768), BF16),
            vm((TO + 1, 480, 128)),
            vm((496, 128)),
            vm((TO, 464, 512), BF16),
            vm((TO, 128, 384), BF16),
            vm((2, 464, 128)),
            vm((2, 464, 128)),
            vm((432, 768), BF16),
            vm((432, 768), BF16),
            vm((T + 1, 432, 256), BF16),
            vm((T + 3, 80, 512)),
            vm((T * 48, 1024), BF16),
            vm((T + 2, 416, 128), BF16),
            vm((T + 2, 48, 416), BF16),
            vm((2, 416, 128)),
            vm((2, 416, 128)),
            vm((384, 768), BF16),
            vm((384, 768), BF16),
            vm((384, 768)),
            vm((144, 256)),
            vm((96, 64)),
            vm((2, 768, 128)),
            vm((480, 128)),
            vm((768, 384), BF16),
            vm((1536, 256), BF16),
            vm((2, 768, 128), BF16),
            vm((TO, 20, 16, 128), BF16),
            vm((1024, 576), BF16),
            pltpu.SemaphoreType.DMA((4,)),
        ],
        compiler_params=pltpu.CompilerParams(vmem_limit_bytes=60 * 1024 * 1024),
        cost_estimate=pl.CostEstimate(flops=10**10, bytes_accessed=2 * 10**7, transcendentals=0),
    )(*args)


def swapped(to_next, to_prev, axis):
    size = lax.axis_size(axis)
    ring = [(i, (i + 1) % size) for i in range(size)]
    return lax.ppermute(to_next, axis, ring), lax.ppermute(to_prev, axis, [(j, i) for i, j in ring])


def packed(clip_part, up_part):
    flat = clip_part.reshape(408, clip_part.shape[3])
    flat = jnp.pad(flat, ((0, 0), (0, 128 - flat.shape[1])))
    return jnp.concatenate([flat, up_part.reshape(-1, 128)], axis=0)


def body(clip, w_first, b_first, w_second, b_second, upstream):
    rows = clip.shape[2] * lax.axis_size("ha")
    cols = clip.shape[3] * lax.axis_size("wa")
    ha, wa = lax.axis_index("ha"), lax.axis_index("wa")
    pos = jnp.stack([ha * 32, wa * 32, jnp.int32(rows), jnp.int32(cols)]).astype(jnp.int32)

    above, below = swapped(
        packed(clip[:, :, 24:32], upstream[:, 14:16]), packed(clip[:, :, 0:8], upstream[:, 0:2]), "ha"
    )
    above = jnp.where(ha > 0, above, jnp.zeros_like(above))
    below = jnp.where(ha < lax.axis_size("ha") - 1, below, jnp.zeros_like(below))
    clip_part = lambda v, width: v[:408, :width].reshape(3, T, 8, width)
    clip_rows = jnp.concatenate([clip_part(above, 32), clip, clip_part(below, 32)], axis=2)
    up_part = lambda v: v[408:].reshape(TO, 2, 16, 128)
    up_rows = jnp.concatenate([up_part(above), upstream, up_part(below)], axis=1)
    left, right = swapped(
        packed(jnp.swapaxes(clip_rows[:, :, :, 24:32], 2, 3), jnp.swapaxes(up_rows[:, :, 14:16], 1, 2)),
        packed(jnp.swapaxes(clip_rows[:, :, :, 0:8], 2, 3), jnp.swapaxes(up_rows[:, :, 0:2], 1, 2)),
        "wa",
    )

    w_flat = w_first.reshape(81, 64)
    diagonal = jnp.concatenate(
        [jnp.pad(w_flat, ((0, 0), (64 * k, 192 - 64 * k))) for k in range(4)], axis=0
    )
    forward_pick = jnp.asarray(first_forward(), BF16)
    w1 = jnp.concatenate(
        [dot(forward_pick[:, e], diagonal).astype(BF16) for e in range(2)], axis=1
    )
    wx = jnp.einsum(
        "ko,bkl->lbo", w_flat, jnp.asarray(first_backward(), BF16), preferred_element_type=F32
    )
    wx = wx.astype(BF16).reshape(80, 1024)
    middle, first8, last8 = pick_columns()
    input_grad, terms = run_kernel(
        pos,
        clip_rows,
        left,
        right,
        up_rows,
        jnp.asarray(middle, BF16),
        jnp.asarray(np.concatenate([first8, last8], axis=1), BF16),
        jnp.asarray(spread_rows(), BF16),
        w1,
        b_first[None],
        w_second.reshape(27, 64, 128),
        b_second[None],
        wx,
        jnp.asarray(place_columns(), BF16),
    )

    scale = 1.0 / (T * rows * cols)
    terms = lax.all_to_all(terms, "wa", 0, 0, tiled=True)
    terms = terms.astype(F32).sum(0)
    step = 1
    while step < lax.axis_size("ha"):
        sent = terms.astype(BF16)
        pairs = [(i, i ^ step) for i in range(lax.axis_size("ha"))]
        terms = sent.astype(F32) + lax.ppermute(sent, "ha", pairs).astype(F32)
        step *= 2
    terms = terms * scale
    lane = lax.broadcasted_iota(jnp.int32, (128, 16), 0)
    mine = lax.broadcasted_iota(jnp.int32, (128, 16), 1)
    pick = (lane == (mine // 8) * 64 + ha * 8 + mine % 8).astype(F32)
    second = jnp.dot(terms[0:120], pick, precision=lax.Precision.HIGHEST, preferred_element_type=F32)
    second = second.reshape(5, 3, 8, 2, 8)
    keep = [TAPS.index((b, c)) for b in range(3) for c in range(3)]
    second = second.transpose(0, 3, 1, 4, 2).reshape(10, 3, 8, 8)
    grad_second = jnp.stack([second[k] for k in keep], axis=1).reshape(3, 3, 3, 8, 8)
    first = terms[96:160]
    grad_first = jnp.concatenate([first[0:24, 0:64], first[24:53, 0:64], first[24:53, 64:128]], axis=0)
    grad_first = grad_first[:81].reshape(3, 3, 3, 3, 64)
    return (input_grad, grad_first, grad_second)


def solution(mesh):
    placed = (P(None, None, "ha", "wa"), P(), P(), P(), P(), P(None, "ha", "wa", None))
    return jax.shard_map(
        body,
        mesh=mesh,
        in_specs=placed,
        out_specs=(P(None, None, "ha", "wa"), P(), P(None, None, None, "ha", "wa")),
        check_vma=False,
    )
```
